256 devices in a mesh: ctx: 64 (over x, z, core), fsdp: 4 (over y).
Axes of the slice: x: 4, y: 4, z: 8, core: 2. Of those that a mesh axis runs over, the one named last changes fastest.
Arguments:
- acts: bfloat16 [131072, 4096], P(('ctx', 'fsdp')), may hold values from -64 to 64
- queries: bfloat16 [131072, 2048], P(('ctx', 'fsdp')), may hold values from -120 to 120
- kv_weight: bfloat16 [4096, 4, 2, 128], P(None, 'fsdp'), may hold values from -1 to 1
- rand_blocks: int32 [1024, 3], replicated, may hold values from 0 to 1023, as said below
Outputs:
- attended: bfloat16 [131072, 2048], P(('ctx', 'fsdp'))
The draws below stay inside these ranges and needn't reach their ends.
Inputs may be any that keep to these rules, and one draw needn't show every extreme that they name: `rand_blocks`: call the 16 consecutive blocks of one index of ctx a context shard. Among the 48 entries of the rows of one context shard, the blocks of any one context shard are named at most 1 times in all, and some context shard is named exactly 1 times.
All inputs are finite; a program needn't handle non-finite values.
Results may differ from the reference program's by a relative error of at most 0.0086.
Values may be sent and summed in bfloat16 or wider, within the bound.
A program may use at most 128 MiB of HBM per device.

```python
import math
import jax
import jax.numpy as jnp
from jax import lax

MODEL_DIM = 4096
QUERY_HEADS = 16
KEY_VALUE_HEADS = 4
HEAD_DIM = 128
BLOCK = 128
GLOBAL = 2
RAND = 3
TOK_DEV = 512
NB = 1024
CAP = 1
N_CTX = 64
N_FSDP = 4


def common_weight(key):
    random_draws = jax.random.normal(jax.random.fold_in(key, 7), (MODEL_DIM, KEY_VALUE_HEADS, 2, HEAD_DIM), jnp.float32)
    return jnp.clip(random_draws, -6.0, 6.0) / math.sqrt(MODEL_DIM)


def draw_acts(key, part):
    random_draws = jnp.clip(jax.random.normal(jax.random.fold_in(key, 3), (NB, BLOCK, MODEL_DIM), jnp.float32), -6.0, 6.0)
    return random_draws.reshape(NB * BLOCK, MODEL_DIM).astype(jnp.bfloat16)


def draw_queries(key, part):
    random_draws = jnp.clip(jax.random.normal(jax.random.fold_in(key, 5), (NB, BLOCK, QUERY_HEADS, HEAD_DIM), jnp.float32), -6.0, 6.0)
    return random_draws.reshape(NB * BLOCK, QUERY_HEADS * HEAD_DIM).astype(jnp.bfloat16)


def draw_kv_weight(key, part):
    return common_weight(key).astype(jnp.bfloat16)


def draw_rand_blocks(key, part):
    shard_count = TOK_DEV * N_FSDP // BLOCK
    entries = shard_count * RAND
    shard_keys = jax.random.split(jax.random.fold_in(key, 9), N_CTX)
    source_pool = jnp.arange(N_CTX * CAP, dtype=jnp.int32) % N_CTX

    def draw_shard(shard_key):
        shuffled = jax.random.permutation(shard_key, N_CTX * CAP)
        return source_pool[shuffled[:entries]]
    sources = jax.vmap(draw_shard)(shard_keys)
    offsets = jax.random.randint(jax.random.fold_in(key, 10), (N_CTX, entries), 0, shard_count, dtype=jnp.int32)
    return (sources * shard_count + offsets).reshape(NB, RAND).astype(jnp.int32)


def setup_inputs(seed: int = 0) -> dict:
    key_list = jax.random.split(jax.random.key(seed), 5)
    return {
        "acts": draw_acts(jax.random.fold_in(key_list[4], 71), 0),
        "queries": draw_queries(jax.random.fold_in(key_list[4], 71), 0),
        "kv_weight": draw_kv_weight(jax.random.fold_in(key_list[4], 71), 0),
        "rand_blocks": draw_rand_blocks(jax.random.fold_in(key_list[4], 71), 0),
    }


def reference(acts, queries, kv_weight, rand_blocks):
    token_count = acts.shape[0]
    block_count = token_count // BLOCK
    kv_heads = kv_weight.shape[1]
    head_size = kv_weight.shape[3]
    group_size = queries.shape[1] // head_size // kv_heads
    flat_weight = kv_weight.reshape(MODEL_DIM, kv_heads * 2 * head_size)

    def project(block_rows):
        return jnp.dot(block_rows, flat_weight, preferred_element_type=jnp.float32).astype(jnp.bfloat16)
    key_value = lax.map(project, acts.reshape(block_count, BLOCK, MODEL_DIM))
    key_value = key_value.reshape(block_count, BLOCK, kv_heads, 2, head_size)
    block_ids = jnp.arange(block_count, dtype=jnp.int32)
    fixed_lists = [(block_ids + block_count - 1) % block_count, block_ids, (block_ids + 1) % block_count]
    for global_id in range(GLOBAL):
        fixed_lists.append(jnp.full((block_count,), global_id, dtype=jnp.int32))
    key_ids = jnp.concatenate([jnp.stack(fixed_lists, axis=1), rand_blocks.astype(jnp.int32)], axis=1)
    query_blocks = queries.reshape(block_count, BLOCK, kv_heads, group_size, head_size)
    scale = 1.0 / math.sqrt(head_size)

    def attend(operands):
        query_part, row_ids = operands
        chosen = key_value[row_ids]
        key_rows = chosen[:, :, :, 0, :].reshape(-1, kv_heads, head_size).astype(jnp.float32)
        values = chosen[:, :, :, 1, :].reshape(-1, kv_heads, head_size).astype(jnp.float32)
        scores = jnp.einsum('qhgd,khd->hgqk', query_part.astype(jnp.float32), key_rows) * scale
        largest = lax.optimization_barrier(jnp.max(scores, axis=-1, keepdims=True))
        weights = jnp.exp(scores - largest)
        probs = (weights / lax.optimization_barrier(jnp.sum(weights, axis=-1, keepdims=True))).astype(jnp.bfloat16)
        result = jnp.einsum('hgqk,khd->qhgd', probs.astype(jnp.float32), values)
        return result.astype(jnp.bfloat16).reshape(BLOCK, kv_heads * group_size * head_size)
    attended = lax.map(attend, (query_blocks, key_ids))
    return attended.reshape(token_count, kv_heads * group_size * head_size)
```

```python
import math

import jax
import jax.numpy as jnp
from jax import lax
from jax.experimental import pallas as pl
from jax.experimental.pallas import tpu as pltpu
from jax.sharding import PartitionSpec as P

BLOCK = 128
RAND = 3
NX, NZ, NY = 4, 8, 4
N_CTX = NX * NZ * 2
SHARD = 16
HEAD = 128
MODEL = 4096
TOK = 512
GROUP = 4
ROW = 2 * HEAD
QCOL = GROUP * HEAD
QUARTER = MODEL // 4
SUB = QUARTER // 4
SLOTS = 59
EXP2_SCALE = math.log2(math.e) / math.sqrt(HEAD)
NT = (((1,), (1,)), ((), ()))


def kernel(
    table, rand, acts, queries, weight, out,
    acts_v, wbuf, kv_send, kv, kvw, glob, before1, after1, before2, after2,
    stage, pool, qx, acc, top, total, outbox,
    loc, wy_s, wy_r, wd_s, wd_r, wx_s, wx_r, kv_s, kv_r, q_s, q_r,
    m_s, m_r, st_s, pool_r, halo_s, halo_r, g_s, g_r, out_s, out_r,
):
    c = lax.axis_index("ctx")
    y = lax.axis_index("fsdp")
    x = c // (2 * NZ)
    z = (c // 2) % NZ
    k = c % 2
    parity = (x + z) % 2

    def at(dx, dz, dk):
        return (((x + dx) % NX) * NZ + (z + dz) % NZ) * 2 + (k + dk) % 2

    def remote(src, dst, send, recv, ctx, head):
        return pltpu.make_async_remote_copy(
            src_ref=src, dst_ref=dst, send_sem=send, recv_sem=recv,
            device_id=(ctx, head), device_id_type=pl.DeviceIdType.MESH,
        )

    def peer(off):
        return (y + off) % NY

    sends = []

    def go(copy):
        copy.start()
        sends.append(copy)

    mine = (parity * 2 + k) * QUARTER
    other = ((1 - parity) * 2 + k) * QUARTER
    whole = pl.ds(mine, QUARTER)
    first = pl.ds(mine, QUARTER // 2)
    second = pl.ds(mine + QUARTER // 2, QUARTER // 2)
    for n, off in enumerate((1, 3)):
        go(remote(weight.at[whole], wbuf.at[y, whole], wy_s.at[n], wy_r.at[n], c, peer(off)))
    acts_in = pltpu.make_async_copy(acts, acts_v, loc.at[0])
    acts_in.start()
    own_w = pltpu.make_async_copy(weight, wbuf.at[y], loc.at[1])
    own_w.start()
    own_q = pltpu.make_async_copy(
        queries.at[:, pl.ds(pl.multiple_of(y * QCOL, QCOL), QCOL)],
        qx.at[pl.ds(y * TOK, TOK)], loc.at[2],
    )
    own_q.start()
    acts_in.wait()
    own_w.wait()

    def project(head, dest, lead):
        def tile(t, _):
            rows = pl.ds(t * 256, 256)
            total_ = jnp.dot(acts_v[rows, 0:1024], wbuf[head, 0:1024],
                             preferred_element_type=jnp.float32)
            for u in range(1, 4):
                total_ += jnp.dot(acts_v[rows, u * 1024:(u + 1) * 1024],
                                  wbuf[head, u * 1024:(u + 1) * 1024],
                                  preferred_element_type=jnp.float32)
            dest[pl.ds(lead + t * 2, 2)] = total_.astype(jnp.bfloat16).reshape(2, BLOCK, ROW)
            return 0
        lax.fori_loop(0, 2, tile, 0)

    project(y, kv, y * 4)

    def multicast(n, head):
        rows = pl.ds(head * 4, 4)
        go(remote(kv.at[rows], before1.at[rows], m_s.at[0, n], m_r.at[0, n], at(0, 1, 0), y))
        go(remote(kv.at[rows], after1.at[rows], m_s.at[1, n], m_r.at[1, n], at(0, -1 + NZ, 0), y))

    def spread(n, off):
        head = peer(off)
        go(remote(wbuf.at[head, whole], wbuf.at[head, whole], wd_s.at[0, n], wd_r.at[0, n],
                  at(0, 0, 1), y))
        for j, (dx, dz) in enumerate(((1, 0), (NX - 1, 0), (0, 1), (0, NZ - 1))):
            rows = pl.ds(mine + j * SUB, SUB)
            go(remote(wbuf.at[head, rows], wbuf.at[head, rows], wx_s.at[n, j], wx_r.at[n, j],
                      at(dx, dz, 0), y))

    def landed(view, send, recv):
        remote(view, view, send, recv, at(0, 0, 1), y).wait_recv()

    landed(wbuf.at[peer(3), whole], wy_s.at[0], wy_r.at[0])
    go(remote(wbuf.at[peer(3), first], wbuf.at[peer(3), first], wy_s.at[2], wy_r.at[2], c, peer(1)))
    landed(wbuf.at[peer(1), whole], wy_s.at[1], wy_r.at[1])
    go(remote(wbuf.at[peer(1), second], wbuf.at[peer(1), second], wy_s.at[3], wy_r.at[3], c, peer(3)))
    spread(0, 1)
    spread(1, 3)
    multicast(0, y)
    landed(wbuf.at[peer(2), first], wy_s.at[2], wy_r.at[2])
    landed(wbuf.at[peer(2), second], wy_s.at[3], wy_r.at[3])
    spread(2, 2)

    offs = (1, 3, 2)
    far = pl.ds(other, QUARTER)
    sib_mine = pl.ds((parity * 2 + 1 - k) * QUARTER, QUARTER)
    sib_other = pl.ds(((1 - parity) * 2 + 1 - k) * QUARTER, QUARTER)
    for n, off in enumerate(offs):
        head = peer(off)
        for j in range(4):
            landed(wbuf.at[head, pl.ds(other + j * SUB, SUB)], wx_s.at[n, j], wx_r.at[n, j])
        go(remote(wbuf.at[head, far], wbuf.at[head, far], wd_s.at[1, n], wd_r.at[1, n],
                  at(0, 0, 1), y))
        landed(wbuf.at[head, sib_mine], wd_s.at[0, n], wd_r.at[0, n])
        landed(wbuf.at[head, sib_other], wd_s.at[1, n], wd_r.at[1, n])
        project(head, kv_send.at[n], 0)
        go(remote(kv_send.at[n], kv.at[pl.ds(y * 4, 4)], kv_s.at[n], kv_r.at[n], c, head))

    for n, off in enumerate(offs):
        head = peer(NY - off)
        landed(kv.at[pl.ds(head * 4, 4)], kv_s.at[n], kv_r.at[n])
        multicast(n + 1, head)

    go(remote(kv.at[SHARD - 1], kvw.at[0], halo_s.at[0], halo_r.at[0], (c + 1) % N_CTX, y))
    go(remote(kv.at[0], kvw.at[SHARD + 1], halo_s.at[1], halo_r.at[1], (c + N_CTX - 1) % N_CTX, y))
    to_window = pltpu.make_async_copy(kv, kvw.at[pl.ds(1, SHARD)], loc.at[3])
    to_window.start()
    to_glob = pltpu.make_async_copy(kv.at[pl.ds(0, 2)], glob, loc.at[4])

    @pl.when(c == 0)
    def _():
        for j in range(1, NZ):
            remote(kv.at[pl.ds(0, 2)], glob, g_s.at[j - 1], g_r, at(0, j, 0), y).start()
        to_glob.start()

    for n, off in enumerate(offs):
        head = peer(off)
        go(remote(queries.at[:, pl.ds(pl.multiple_of(head * QCOL, QCOL), QCOL)],
                  qx.at[pl.ds(y * TOK, TOK)], q_s.at[n], q_r.at[n], c, head))

    def pick_to(source, buffer, base, lo, hi, dest_of):
        def body(n, _):
            dst = dest_of(n)
            slot = base + n - lo
            stage[slot] = buffer[table[dst * N_CTX + source]]
            remote(stage.at[slot], pool.at[source], st_s, pool_r, dst, y).start()
            return 0
        lax.fori_loop(lo, hi, body, 0)

    def plane(source, buffer, base):
        pool[source] = buffer[table[c * N_CTX + source]]
        pick_to(source, buffer, base, 1, 8, lambda n: at(n // 2, 0, n % 2))

    plane(c, kv, 0)

    below, above = at(0, NZ - 1, 0), at(0, 1, 0)
    for n, off in enumerate((0, *offs)):
        rows = pl.ds(peer(NY - off) * 4, 4)
        landed(before1.at[rows], m_s.at[0, n], m_r.at[0, n])
        go(remote(before1.at[rows], before2.at[rows], m_s.at[2, n], m_r.at[2, n], above, y))
        landed(after1.at[rows], m_s.at[1, n], m_r.at[1, n])
        go(remote(after1.at[rows], after2.at[rows], m_s.at[3, n], m_r.at[3, n], below, y))
    plane(below, before1, 7)
    plane(above, after1, 14)

    @pl.when(c == 0)
    def _():
        to_glob.wait()

    @pl.when(c != 0)
    def _():
        landed(glob, g_s.at[0], g_r)

    on_line = jnp.logical_and(x == 0, k == 0)

    @pl.when(on_line)
    def _():
        for j in range(1, 8):
            remote(glob, glob, g_s.at[6 + j], g_r, at(j // 2, 0, j % 2), y).start()

    to_window.wait()
    landed(kvw.at[0], halo_s.at[0], halo_r.at[0])
    landed(kvw.at[SHARD + 1], halo_s.at[1], halo_r.at[1])
    own_q.wait()
    for n, off in enumerate(offs):
        landed(qx.at[pl.ds(peer(NY - off) * TOK, TOK)], q_s.at[n], q_r.at[n])

    half = GROUP // 2

    def stacked(i, part):
        rows = pl.ds(i * BLOCK, BLOCK)
        return jnp.concatenate(
            [qx[rows, g * HEAD:(g + 1) * HEAD] for g in range(part * half, (part + 1) * half)], axis=0
        )

    def near(i, _):
        keys = jnp.concatenate(
            [kvw[pl.ds(i, 3), :, 0:HEAD].reshape(3 * BLOCK, HEAD),
             glob[:, :, 0:HEAD].reshape(2 * BLOCK, HEAD)], axis=0)
        values = jnp.concatenate(
            [kvw[pl.ds(i, 3), :, HEAD:ROW].reshape(3 * BLOCK, HEAD),
             glob[:, :, HEAD:ROW].reshape(2 * BLOCK, HEAD)], axis=0)
        for part in range(2):
            rows = slice(part * half * BLOCK, (part + 1) * half * BLOCK)
            scores = lax.dot_general(stacked(i, part), keys, NT, preferred_element_type=jnp.float32)
            largest = jnp.max(scores, axis=-1, keepdims=True)
            weights = jnp.exp2((scores - largest) * EXP2_SCALE)
            top[i, rows] = largest
            total[i, rows] = jnp.sum(weights, axis=-1, keepdims=True)
            acc[i, rows] = jnp.dot(weights.astype(jnp.bfloat16), values,
                                   preferred_element_type=jnp.float32)
        return 0

    lax.fori_loop(0, 8, near, 0)

    for n, off in enumerate((0, *offs)):
        rows = pl.ds(peer(NY - off) * 4, 4)
        landed(before2.at[rows], m_s.at[2, n], m_r.at[2, n])
        landed(after2.at[rows], m_s.at[3, n], m_r.at[3, n])
    below2, above2 = at(0, NZ - 2, 0), at(0, 2, 0)
    pick_to(below2, before2, 21, 0, 4, lambda n: at(n, 2, 0))
    pick_to(above2, after2, 25, 0, 4, lambda n: at(n, NZ - 2, 1))
    pick_to(below2, before2, 29, 0, 8, lambda n: at(n // 2, 1, n % 2))
    pick_to(above2, after2, 37, 0, 8, lambda n: at(n // 2, NZ - 1, n % 2))
    plane(below2, before2, 45)
    plane(above2, after2, 52)

    lax.fori_loop(8, 16, near, 0)

    landed(pool.at[pl.ds(0, SLOTS)], st_s, pool_r)

    def out_copy(j, i):
        column = pl.ds(pl.multiple_of(y * QCOL, QCOL), QCOL)
        return remote(outbox.at[pl.ds(i * BLOCK, BLOCK)],
                      out.at[pl.ds((i % 4) * BLOCK, BLOCK), column],
                      out_s.at[j], out_r.at[j], c, i // 4)

    def out_local(j, i):
        column = pl.ds(pl.multiple_of(y * QCOL, QCOL), QCOL)
        return pltpu.make_async_copy(outbox.at[pl.ds(i * BLOCK, BLOCK)],
                                     out.at[pl.ds((i % 4) * BLOCK, BLOCK), column], out_s.at[j])

    def block_of(j):
        step = j // 4
        off = jnp.where(step < 2, 2 - step, (3 - step) * 3)
        return ((y + off) % NY) * 4 + j % 4

    def finish(j, _):
        i = block_of(j)
        entry = (c * SHARD + i) * RAND
        chosen = [pool[rand[entry + r] // SHARD] for r in range(RAND)]
        keys = jnp.concatenate([b[:, 0:HEAD] for b in chosen], axis=0)
        values = jnp.concatenate([b[:, HEAD:ROW] for b in chosen], axis=0)
        for part in range(2):
            rows = slice(part * half * BLOCK, (part + 1) * half * BLOCK)
            scores = lax.dot_general(stacked(i, part), keys, NT, preferred_element_type=jnp.float32)
            early = top[i, rows]
            largest = jnp.maximum(early, jnp.max(scores, axis=-1, keepdims=True))
            weights = jnp.exp2((scores - largest) * EXP2_SCALE)
            fade = jnp.exp2((early - largest) * EXP2_SCALE)
            mass = total[i, rows] * fade + jnp.sum(weights, axis=-1, keepdims=True)
            mixed = acc[i, rows] * fade + jnp.dot(weights.astype(jnp.bfloat16), values,
                                                  preferred_element_type=jnp.float32)
            result = (mixed / mass).astype(jnp.bfloat16)
            for g in range(half):
                column = (part * half + g) * HEAD
                outbox[pl.ds(i * BLOCK, BLOCK), column:column + HEAD] = result[g * BLOCK:(g + 1) * BLOCK]

        @pl.when(j < 12)
        def _():
            out_copy(j, i).start()

        @pl.when(j >= 12)
        def _():
            out_local(j, i).start()
        return 0

    lax.fori_loop(0, 16, finish, 0)

    for copy in sends:
        copy.wait_send()

    @pl.when(c == 0)
    def _():
        for j in range(1, NZ):
            remote(kv.at[pl.ds(0, 2)], glob, g_s.at[j - 1], g_r, at(0, j, 0), y).wait_send()

    @pl.when(on_line)
    def _():
        for j in range(1, 8):
            remote(glob, glob, g_s.at[6 + j], g_r, at(j // 2, 0, j % 2), y).wait_send()

    everything = stage.at[pl.ds(0, SLOTS)]
    remote(everything, pool.at[pl.ds(0, SLOTS)], st_s, pool_r, at(0, 0, 1), y).wait_send()

    def drain(j, _):
        i = block_of(j)

        @pl.when(j < 12)
        def _():
            out_copy(j, i).wait()

        @pl.when(j >= 12)
        def _():
            out_local(j, i).wait()
        return 0

    lax.fori_loop(0, 16, drain, 0)


def shards(acts, queries, kv_weight, rand_blocks):
    flat_weight = kv_weight.reshape(MODEL, ROW)
    requests = rand_blocks.reshape(N_CTX, SHARD * RAND)
    holder = jnp.arange(N_CTX, dtype=jnp.int32)
    named = (requests // SHARD)[:, :, None] == holder[None, None, :]
    table = jnp.sum(jnp.where(named, (requests % SHARD)[:, :, None], 0), axis=1).astype(jnp.int32)
    bf16, f32 = jnp.bfloat16, jnp.float32
    blocks = pltpu.VMEM((SHARD, BLOCK, ROW), bf16)
    dma = pltpu.SemaphoreType.DMA
    return pl.pallas_call(
        kernel,
        out_shape=jax.ShapeDtypeStruct((TOK, NY * QCOL), bf16),
        in_specs=[pl.BlockSpec(memory_space=pltpu.SMEM)] * 2 + [pl.BlockSpec(memory_space=pl.ANY)] * 3,
        out_specs=pl.BlockSpec(memory_space=pl.ANY),
        scratch_shapes=[
            pltpu.VMEM((TOK, MODEL), bf16),
            pltpu.VMEM((NY, MODEL, ROW), bf16),
            pltpu.VMEM((3, 4, BLOCK, ROW), bf16),
            blocks,
            pltpu.VMEM((SHARD + 2, BLOCK, ROW), bf16),
            pltpu.VMEM((2, BLOCK, ROW), bf16),
            blocks, blocks, blocks, blocks,
            pltpu.VMEM((SLOTS, BLOCK, ROW), bf16),
            pltpu.VMEM((N_CTX, BLOCK, ROW), bf16),
            pltpu.VMEM((NY * TOK, QCOL), bf16),
            pltpu.VMEM((SHARD, GROUP * BLOCK, HEAD), f32),
            pltpu.VMEM((SHARD, GROUP * BLOCK, 1), f32),
            pltpu.VMEM((SHARD, GROUP * BLOCK, 1), f32),
            pltpu.VMEM((NY * TOK, QCOL), bf16),
            dma((5,)), dma((4,)), dma((4,)), dma((2, 3)), dma((2, 3)), dma((3, 4)), dma((3, 4)),
            dma((3,)), dma((3,)), dma((3,)), dma((3,)),
            dma((4, 4)), dma((4, 4)), dma, dma, dma((2,)), dma((2,)), dma((14,)), dma,
            dma((16,)), dma((16,)),
        ],
        compiler_params=pltpu.CompilerParams(
            has_side_effects=True, vmem_limit_bytes=60 * 1024 * 1024
        ),
        cost_estimate=pl.CostEstimate(
            flops=9 * 10**9, bytes_accessed=12 * 2**20, transcendentals=8 * 2**20
        ),
    )(table.reshape(-1), rand_blocks.reshape(-1), acts, queries, flat_weight)


def solution(mesh):
    placed = (P(("ctx", "fsdp"), None), P(("ctx", "fsdp"), None), P(None, "fsdp", None, None), P())
    return jax.shard_map(
        shards, mesh=mesh, in_specs=placed, out_specs=P(("ctx", "fsdp"), None), check_vma=False
    )
```

```python
import math

import jax
import jax.numpy as jnp
from jax import lax
from jax.experimental import pallas as pl
from jax.experimental.pallas import tpu as pltpu
from jax.sharding import PartitionSpec as P

BLOCK = 128
RAND = 3
NX, NZ, NY = 4, 8, 4
N_CTX = NX * NZ * 2
SHARD = 16
HEAD = 128
MODEL = 4096
TOK = 512
GROUP = 4
ROW = 2 * HEAD
QCOL = GROUP * HEAD
QUARTER = MODEL // 4
SUB = QUARTER // 4
SLOTS = 59
EXP2_SCALE = math.log2(math.e) / math.sqrt(HEAD)
NT = (((1,), (1,)), ((), ()))


def kernel(
    rand, acts, queries, weight, out,
    acts_v, wbuf, kv_send, kv, kvw, glob, before1, after1, before2, after2,
    stage, pool, qx, acc, top, total, outbox, table, pairs,
    loc, wy_s, wy_r, wd_s, wd_r, wx_s, wx_r, kv_s, kv_r, q_s, q_r,
    m_s, m_r, st_s, pool_r, halo_s, halo_r, g_s, g_r, out_s, out_r,
):
    c = lax.axis_index("ctx")
    y = lax.axis_index("fsdp")
    x = c // (2 * NZ)
    z = (c // 2) % NZ
    k = c % 2
    parity = (x + z) % 2

    def at(dx, dz, dk):
        return (((x + dx) % NX) * NZ + (z + dz) % NZ) * 2 + (k + dk) % 2

    def remote(src, dst, send, recv, ctx, head):
        return pltpu.make_async_remote_copy(
            src_ref=src, dst_ref=dst, send_sem=send, recv_sem=recv,
            device_id=(ctx, head), device_id_type=pl.DeviceIdType.MESH,
        )

    def peer(off):
        return (y + off) % NY

    sends = []

    def go(copy):
        copy.start()
        sends.append(copy)

    mine = (parity * 2 + k) * QUARTER
    other = ((1 - parity) * 2 + k) * QUARTER
    whole = pl.ds(mine, QUARTER)
    first = pl.ds(mine, QUARTER // 2)
    second = pl.ds(mine + QUARTER // 2, QUARTER // 2)
    barrier = pltpu.get_barrier_semaphore()

    def greet(ctx, head):
        pl.semaphore_signal(barrier, inc=1, device_id=(ctx, head), device_id_type=pl.DeviceIdType.MESH)

    for off in range(1, NY):
        greet(c, peer(off))
    for dz in (1, NZ - 1, 2, NZ - 2):
        greet(at(0, dz, 0), y)
    for n in range(1, 8):
        greet(at(n // 2, 0, n % 2), y)
    own_w = pltpu.make_async_copy(weight, pairs, loc.at[1])
    own_w.start()
    own_q = pltpu.make_async_copy(
        queries.at[:, pl.ds(pl.multiple_of(y * QCOL, QCOL), QCOL)],
        qx.at[pl.ds(y * TOK, TOK)], loc.at[2],
    )
    acts_in = pltpu.make_async_copy(acts, acts_v, loc.at[0])
    acts_in.start()
    own_q.start()
    own_w.wait()

    line = lax.broadcasted_iota(jnp.int32, (2 * BLOCK, 2 * BLOCK), 0)
    place = lax.broadcasted_iota(jnp.int32, (2 * BLOCK, 2 * BLOCK), 1)
    wanted = jnp.where(line < BLOCK, 2 * line, 2 * (line - BLOCK) + 1)
    order = jnp.where(place == wanted, 1.0, 0.0).astype(jnp.bfloat16)

    def set_apart(b, _):
        parts = jnp.dot(order, pairs[pl.ds(b * ROW, ROW)], preferred_element_type=jnp.float32)
        parts = parts.astype(jnp.bfloat16)
        rows = pl.ds(b * BLOCK, BLOCK)
        wbuf[y, rows, 0:HEAD] = parts[0:BLOCK]
        wbuf[y, rows, HEAD:ROW] = parts[BLOCK:2 * BLOCK]
        return 0

    lax.fori_loop(0, MODEL // BLOCK, set_apart, 0, unroll=4)
    pl.semaphore_wait(barrier, 14)
    for n, off in enumerate((1, 3)):
        go(remote(wbuf.at[y, whole], wbuf.at[y, whole], wy_s.at[n], wy_r.at[n], c, peer(off)))
    acts_in.wait()

    def project(head, dest, lead):
        def tile(t, _):
            rows = pl.ds(t * 256, 256)
            total_ = jnp.dot(acts_v[rows, 0:1024], wbuf[head, 0:1024],
                             preferred_element_type=jnp.float32)
            for u in range(1, 4):
                total_ += jnp.dot(acts_v[rows, u * 1024:(u + 1) * 1024],
                                  wbuf[head, u * 1024:(u + 1) * 1024],
                                  preferred_element_type=jnp.float32)
            dest[pl.ds(lead + t * 2, 2)] = total_.astype(jnp.bfloat16).reshape(2, BLOCK, ROW)
            return 0
        lax.fori_loop(0, 2, tile, 0)

    project(y, kv, y * 4)

    offs = (1, 3, 2)

    def landed(view, send, recv):
        remote(view, view, send, recv, at(0, 0, 1), y).wait_recv()

    below, above = at(0, NZ - 1, 0), at(0, 1, 0)
    below2, above2 = at(0, NZ - 2, 0), at(0, 2, 0)

    def in_plane(n):
        return at(n // 2, 0, n % 2)

    groups = {
        "own": (c, 0, 1, 8, in_plane),
        "below": (below, 7, 1, 8, in_plane),
        "above": (above, 14, 1, 8, in_plane),
        "below2 far": (below2, 21, 0, 4, lambda n: at(n, 2, 0)),
        "above2 far": (above2, 25, 0, 4, lambda n: at(n, NZ - 2, 1)),
        "below2 next": (below2, 29, 0, 8, lambda n: at(n // 2, 1, n % 2)),
        "above2 next": (above2, 37, 0, 8, lambda n: at(n // 2, NZ - 1, n % 2)),
        "below2": (below2, 45, 1, 8, in_plane),
        "above2": (above2, 52, 1, 8, in_plane),
    }
    keep = {"own": 59, "below": 60, "above": 61, "below2": 62, "above2": 63}

    def named_block(dst, source):
        found = jnp.int32(0)
        for r in range(RAND):
            for b in range(SHARD):
                v = rand[r * N_CTX * SHARD + dst * SHARD + b]
                found += jnp.where(v >> 4 == source, v & 15, 0)
        return found

    def look_up(name):
        source, base, lo, hi, dest_of = groups[name]

        def body(n, _):
            table[base + n - lo] = named_block(dest_of(n), source)
            return 0

        lax.fori_loop(lo, hi, body, 0)
        if name in keep:
            table[keep[name]] = named_block(c, source)

    def pick(name, buffer):
        source, base, lo, hi, dest_of = groups[name]
        if name in keep:
            pool[source] = buffer[table[keep[name]]]

        def body(n, _):
            slot = base + n - lo
            stage[slot] = buffer[table[slot]]
            remote(stage.at[slot], pool.at[source], st_s, pool_r, dest_of(n), y).start()
            return 0

        lax.fori_loop(lo, hi, body, 0)

    def forward(n):
        rows = pl.ds(peer(NY - (0, *offs)[n]) * 4, 4)
        landed(before1.at[rows], m_s.at[0, n], m_r.at[0, n])
        go(remote(before1.at[rows], before2.at[rows], m_s.at[2, n], m_r.at[2, n], above, y))
        landed(after1.at[rows], m_s.at[1, n], m_r.at[1, n])
        go(remote(after1.at[rows], after2.at[rows], m_s.at[3, n], m_r.at[3, n], below, y))

    def multicast(n, head):
        rows = pl.ds(head * 4, 4)
        go(remote(kv.at[rows], before1.at[rows], m_s.at[0, n], m_r.at[0, n], at(0, 1, 0), y))
        go(remote(kv.at[rows], after1.at[rows], m_s.at[1, n], m_r.at[1, n], at(0, -1 + NZ, 0), y))

    def spread(n, off):
        head = peer(off)
        go(remote(wbuf.at[head, whole], wbuf.at[head, whole], wd_s.at[0, n], wd_r.at[0, n],
                  at(0, 0, 1), y))
        for j, (dx, dz) in enumerate(((1, 0), (NX - 1, 0), (0, 1), (0, NZ - 1))):
            rows = pl.ds(mine + j * SUB, SUB)
            go(remote(wbuf.at[head, rows], wbuf.at[head, rows], wx_s.at[n, j], wx_r.at[n, j],
                      at(dx, dz, 0), y))

    multicast(0, y)
    for name in groups:
        look_up(name)

    landed(wbuf.at[peer(3), whole], wy_s.at[0], wy_r.at[0])
    go(remote(wbuf.at[peer(3), first], wbuf.at[peer(3), first], wy_s.at[2], wy_r.at[2], c, peer(1)))
    landed(wbuf.at[peer(1), whole], wy_s.at[1], wy_r.at[1])
    go(remote(wbuf.at[peer(1), second], wbuf.at[peer(1), second], wy_s.at[3], wy_r.at[3], c, peer(3)))
    spread(0, 1)
    spread(1, 3)
    forward(0)
    landed(wbuf.at[peer(2), first], wy_s.at[2], wy_r.at[2])
    landed(wbuf.at[peer(2), second], wy_s.at[3], wy_r.at[3])
    spread(2, 2)

    far = pl.ds(other, QUARTER)
    sib_mine = pl.ds((parity * 2 + 1 - k) * QUARTER, QUARTER)
    sib_other = pl.ds(((1 - parity) * 2 + 1 - k) * QUARTER, QUARTER)
    for n, off in enumerate(offs):
        head = peer(off)
        for j in range(4):
            landed(wbuf.at[head, pl.ds(other + j * SUB, SUB)], wx_s.at[n, j], wx_r.at[n, j])
        go(remote(wbuf.at[head, far], wbuf.at[head, far], wd_s.at[1, n], wd_r.at[1, n],
                  at(0, 0, 1), y))
        landed(wbuf.at[head, sib_mine], wd_s.at[0, n], wd_r.at[0, n])
        landed(wbuf.at[head, sib_other], wd_s.at[1, n], wd_r.at[1, n])
        project(head, kv_send.at[n], 0)
        go(remote(kv_send.at[n], kv.at[pl.ds(y * 4, 4)], kv_s.at[n], kv_r.at[n], c, head))

    to_glob = pltpu.make_async_copy(kv.at[pl.ds(0, 2)], glob, loc.at[4])

    def root_copies():
        return [remote(kv.at[pl.ds(0, 2)], glob, g_s.at[n], g_r, at(0, dz, 0), y)
                for n, dz in enumerate((2, NZ - 2, 1, NZ - 1))]

    def up_copies():
        return [remote(glob, glob, g_s.at[4 + n], g_r, at(0, dz, 0), y) for n, dz in enumerate((2, 1))]

    def down_copies():
        return [remote(glob, glob, g_s.at[6], g_r, at(0, NZ - 1, 0), y)]

    def plane_copies():
        return [remote(glob, glob, g_s.at[6 + j], g_r, at(j // 2, 0, j % 2), y) for j in range(1, 8)]

    on_line = jnp.logical_and(x == 0, k == 0)
    tree = (
        (jnp.logical_and(on_line, z == 2), up_copies),
        (jnp.logical_and(on_line, z == NZ - 2), down_copies),
        (on_line, plane_copies),
    )

    def send_globals(holder):
        @pl.when(jnp.logical_and(c == 0, holder == 0))
        def _():
            for copy in root_copies():
                copy.start()
            to_glob.start()

    send_globals(y)

    for n, off in enumerate(offs):
        head = peer(NY - off)
        landed(kv.at[pl.ds(head * 4, 4)], kv_s.at[n], kv_r.at[n])
        send_globals(head)
        multicast(n + 1, head)
        if n:
            forward(n)

    @pl.when(c == 0)
    def _():
        to_glob.wait()

    @pl.when(jnp.logical_and(on_line, c != 0))
    def _():
        landed(glob, g_s.at[0], g_r)

    for holds, copies in tree:
        @pl.when(holds)
        def _():
            for copy in copies():
                copy.start()

    go(remote(kv.at[SHARD - 1], kvw.at[0], halo_s.at[0], halo_r.at[0], (c + 1) % N_CTX, y))
    go(remote(kv.at[0], kvw.at[SHARD + 1], halo_s.at[1], halo_r.at[1], (c + N_CTX - 1) % N_CTX, y))
    to_window = pltpu.make_async_copy(kv, kvw.at[pl.ds(1, SHARD)], loc.at[3])
    to_window.start()
    for n, off in enumerate(offs):
        head = peer(off)
        go(remote(queries.at[:, pl.ds(pl.multiple_of(head * QCOL, QCOL), QCOL)],
                  qx.at[pl.ds(y * TOK, TOK)], q_s.at[n], q_r.at[n], c, head))

    pick("own", kv)
    forward(3)
    pick("below", before1)
    pick("above", after1)

    @pl.when(jnp.logical_not(on_line))
    def _():
        landed(glob, g_s.at[0], g_r)

    to_window.wait()
    landed(kvw.at[0], halo_s.at[0], halo_r.at[0])
    landed(kvw.at[SHARD + 1], halo_s.at[1], halo_r.at[1])
    own_q.wait()
    for n, off in enumerate(offs):
        landed(qx.at[pl.ds(peer(NY - off) * TOK, TOK)], q_s.at[n], q_r.at[n])

    half = GROUP // 2

    def stacked(i, part):
        rows = pl.ds(i * BLOCK, BLOCK)
        return jnp.concatenate(
            [qx[rows, g * HEAD:(g + 1) * HEAD] for g in range(part * half, (part + 1) * half)], axis=0
        )

    def near(i, _):
        keys = jnp.concatenate(
            [kvw[pl.ds(i, 3), :, 0:HEAD].reshape(3 * BLOCK, HEAD),
             glob[:, :, 0:HEAD].reshape(2 * BLOCK, HEAD)], axis=0)
        values = jnp.concatenate(
            [kvw[pl.ds(i, 3), :, HEAD:ROW].reshape(3 * BLOCK, HEAD),
             glob[:, :, HEAD:ROW].reshape(2 * BLOCK, HEAD)], axis=0)
        for part in range(2):
            rows = slice(part * half * BLOCK, (part + 1) * half * BLOCK)
            scores = lax.dot_general(stacked(i, part), keys, NT, preferred_element_type=jnp.float32)
            largest = jnp.max(scores, axis=-1, keepdims=True)
            weights = jnp.exp2((scores - largest) * EXP2_SCALE)
            top[i, rows] = largest
            total[i, rows] = jnp.sum(weights, axis=-1, keepdims=True)
            acc[i, rows] = jnp.dot(weights.astype(jnp.bfloat16), values,
                                   preferred_element_type=jnp.float32)
        return 0

    lax.fori_loop(0, 8, near, 0)

    for n, off in enumerate((0, *offs)):
        rows = pl.ds(peer(NY - off) * 4, 4)
        landed(before2.at[rows], m_s.at[2, n], m_r.at[2, n])
        landed(after2.at[rows], m_s.at[3, n], m_r.at[3, n])
    pick("below2 far", before2)
    pick("above2 far", after2)
    pick("below2 next", before2)
    pick("above2 next", after2)
    pick("below2", before2)
    pick("above2", after2)

    lax.fori_loop(8, 16, near, 0)

    landed(pool.at[pl.ds(0, SLOTS)], st_s, pool_r)

    def out_copy(j, i):
        column = pl.ds(pl.multiple_of(y * QCOL, QCOL), QCOL)
        return remote(outbox.at[pl.ds(i * BLOCK, BLOCK)],
                      out.at[pl.ds((i % 4) * BLOCK, BLOCK), column],
                      out_s.at[j], out_r.at[j], c, i // 4)

    def out_local(j, i):
        column = pl.ds(pl.multiple_of(y * QCOL, QCOL), QCOL)
        return pltpu.make_async_copy(outbox.at[pl.ds(i * BLOCK, BLOCK)],
                                     out.at[pl.ds((i % 4) * BLOCK, BLOCK), column], out_s.at[j])

    def block_of(j):
        step = j // 4
        off = jnp.where(step < 2, 2 - step, (3 - step) * 3)
        return ((y + off) % NY) * 4 + j % 4

    def finish(j, _):
        i = block_of(j)
        chosen = [pool[rand[r * N_CTX * SHARD + c * SHARD + i] >> 4] for r in range(RAND)]
        keys = jnp.concatenate([b[:, 0:HEAD] for b in chosen], axis=0)
        values = jnp.concatenate([b[:, HEAD:ROW] for b in chosen], axis=0)
        for part in range(2):
            rows = slice(part * half * BLOCK, (part + 1) * half * BLOCK)
            scores = lax.dot_general(stacked(i, part), keys, NT, preferred_element_type=jnp.float32)
            early = top[i, rows]
            largest = jnp.maximum(early, jnp.max(scores, axis=-1, keepdims=True))
            weights = jnp.exp2((scores - largest) * EXP2_SCALE)
            fade = jnp.exp2((early - largest) * EXP2_SCALE)
            mass = total[i, rows] * fade + jnp.sum(weights, axis=-1, keepdims=True)
            mixed = acc[i, rows] * fade + jnp.dot(weights.astype(jnp.bfloat16), values,
                                                  preferred_element_type=jnp.float32)
            result = (mixed / mass).astype(jnp.bfloat16)
            for g in range(half):
                column = (part * half + g) * HEAD
                outbox[pl.ds(i * BLOCK, BLOCK), column:column + HEAD] = result[g * BLOCK:(g + 1) * BLOCK]

        @pl.when(j < 12)
        def _():
            out_copy(j, i).start()

        @pl.when(j >= 12)
        def _():
            out_local(j, i).start()
        return 0

    lax.fori_loop(0, 16, finish, 0)

    for copy in sends:
        copy.wait_send()

    for holds, copies in ((c == 0, root_copies), *tree):
        @pl.when(holds)
        def _():
            for copy in copies():
                copy.wait_send()

    everything = stage.at[pl.ds(0, SLOTS)]
    remote(everything, pool.at[pl.ds(0, SLOTS)], st_s, pool_r, at(0, 0, 1), y).wait_send()

    def drain(j, _):
        i = block_of(j)

        @pl.when(j < 12)
        def _():
            out_copy(j, i).wait()

        @pl.when(j >= 12)
        def _():
            out_local(j, i).wait()
        return 0

    lax.fori_loop(0, 16, drain, 0)


def shards(acts, queries, kv_weight, rand_blocks):
    flat_weight = kv_weight.reshape(2 * MODEL, HEAD)
    bf16, f32 = jnp.bfloat16, jnp.float32
    blocks = pltpu.VMEM((SHARD, BLOCK, ROW), bf16)
    dma = pltpu.SemaphoreType.DMA
    return pl.pallas_call(
        kernel,
        out_shape=jax.ShapeDtypeStruct((TOK, NY * QCOL), bf16),
        in_specs=[pl.BlockSpec(memory_space=pltpu.SMEM)] + [pl.BlockSpec(memory_space=pl.ANY)] * 3,
        out_specs=pl.BlockSpec(memory_space=pl.ANY),
        scratch_shapes=[
            pltpu.VMEM((TOK, MODEL), bf16),
            pltpu.VMEM((NY, MODEL, ROW), bf16),
            pltpu.VMEM((3, 4, BLOCK, ROW), bf16),
            blocks,
            pltpu.VMEM((SHARD + 2, BLOCK, ROW), bf16),
            pltpu.VMEM((2, BLOCK, ROW), bf16),
            blocks, blocks, blocks, blocks,
            pltpu.VMEM((SLOTS, BLOCK, ROW), bf16),
            pltpu.VMEM((N_CTX, BLOCK, ROW), bf16),
            pltpu.VMEM((NY * TOK, QCOL), bf16),
            pltpu.VMEM((SHARD, GROUP * BLOCK, HEAD), f32),
            pltpu.VMEM((SHARD, GROUP * BLOCK, 1), f32),
            pltpu.VMEM((SHARD, GROUP * BLOCK, 1), f32),
            pltpu.VMEM((NY * TOK, QCOL), bf16),
            pltpu.SMEM((N_CTX,), jnp.int32),
            pltpu.VMEM((2 * MODEL, HEAD), bf16),
            dma((5,)), dma((4,)), dma((4,)), dma((2, 3)), dma((2, 3)), dma((3, 4)), dma((3, 4)),
            dma((3,)), dma((3,)), dma((3,)), dma((3,)),
            dma((4, 4)), dma((4, 4)), dma, dma, dma((2,)), dma((2,)), dma((14,)), dma,
            dma((16,)), dma((16,)),
        ],
        compiler_params=pltpu.CompilerParams(
            collective_id=0, has_side_effects=True, vmem_limit_bytes=60 * 1024 * 1024
        ),
        cost_estimate=pl.CostEstimate(
            flops=9 * 10**9, bytes_accessed=12 * 2**20, transcendentals=8 * 2**20
        ),
    )(rand_blocks.T.reshape(-1), acts, queries, flat_weight)


def solution(mesh):
    placed = (P(("ctx", "fsdp"), None), P(("ctx", "fsdp"), None), P(None, "fsdp", None, None), P())
    return jax.shard_map(
        shards, mesh=mesh, in_specs=placed, out_specs=P(("ctx", "fsdp"), None), check_vma=False
    )
```

```python
import math

import jax
import jax.numpy as jnp
from jax import lax
from jax.experimental import pallas as pl
from jax.experimental.pallas import tpu as pltpu
from jax.sharding import PartitionSpec as P

BLOCK = 128
RAND = 3
NX, NZ, NY = 4, 8, 4
N_CTX = NX * NZ * 2
SHARD = 16
HEAD = 128
MODEL = 4096
TOK = 512
GROUP = 4
ROW = 2 * HEAD
QCOL = GROUP * HEAD
QUARTER = MODEL // 4
SUB = QUARTER // 4
SLOTS = 61
EXP2_SCALE = math.log2(math.e) / math.sqrt(HEAD)
NT = (((1,), (1,)), ((), ()))


def kernel(
    rand, acts, queries, weight, out,
    acts_v, wbuf, kv_send, kv, kvw, glob, before, after,
    stage, pool, qx, acc, top, total, outbox, table, pairs,
    loc, wy_s, wy_r, wd_s, wd_r, wx_s, wx_r, kv_s, kv_r, q_s, q_r,
    m_s, m_r, st_s, pool_r, halo_s, halo_r, g_s, g_r, out_s, out_r, near_by,
):
    c = lax.axis_index("ctx")
    y = lax.axis_index("fsdp")
    x = c // (2 * NZ)
    z = (c // 2) % NZ
    k = c % 2
    parity = (x + z) % 2

    def at(dx, dz, dk):
        return (((x + dx) % NX) * NZ + (z + dz) % NZ) * 2 + (k + dk) % 2

    def remote(src, dst, send, recv, ctx, head):
        return pltpu.make_async_remote_copy(
            src_ref=src, dst_ref=dst, send_sem=send, recv_sem=recv,
            device_id=(ctx, head), device_id_type=pl.DeviceIdType.MESH,
        )

    def peer(off):
        return (y + off) % NY

    sends = []

    def go(copy):
        copy.start()
        sends.append(copy)

    mine = (parity * 2 + k) * QUARTER
    other = ((1 - parity) * 2 + k) * QUARTER
    whole = pl.ds(mine, QUARTER)
    first = pl.ds(mine, QUARTER // 2)
    second = pl.ds(mine + QUARTER // 2, QUARTER // 2)
    barrier = pltpu.get_barrier_semaphore()

    def greet(ctx, head):
        pl.semaphore_signal(barrier, inc=1, device_id=(ctx, head), device_id_type=pl.DeviceIdType.MESH)

    for off in range(1, NY):
        greet(c, peer(off))
    along = (1, NZ - 1, 2, NZ - 2, 3, NZ - 3)
    for dz in along:
        greet(at(0, dz, 0), y)
    for n in range(1, 8):
        greet(at(n // 2, 0, n % 2), y)
    own_w = pltpu.make_async_copy(weight, pairs, loc.at[1])
    own_w.start()
    own_q = pltpu.make_async_copy(
        queries.at[:, pl.ds(pl.multiple_of(y * QCOL, QCOL), QCOL)],
        qx.at[pl.ds(y * TOK, TOK)], loc.at[2],
    )
    acts_in = pltpu.make_async_copy(acts, acts_v, loc.at[0])
    acts_in.start()
    own_q.start()
    own_w.wait()

    line = lax.broadcasted_iota(jnp.int32, (2 * BLOCK, 2 * BLOCK), 0)
    place = lax.broadcasted_iota(jnp.int32, (2 * BLOCK, 2 * BLOCK), 1)
    wanted = jnp.where(line < BLOCK, 2 * line, 2 * (line - BLOCK) + 1)
    order = jnp.where(place == wanted, 1.0, 0.0).astype(jnp.bfloat16)

    def set_apart(b, _):
        parts = jnp.dot(order, pairs[pl.ds(b * ROW, ROW)], preferred_element_type=jnp.float32)
        parts = parts.astype(jnp.bfloat16)
        rows = pl.ds(b * BLOCK, BLOCK)
        wbuf[y, rows, 0:HEAD] = parts[0:BLOCK]
        wbuf[y, rows, HEAD:ROW] = parts[BLOCK:2 * BLOCK]
        return 0

    lax.fori_loop(0, MODEL // BLOCK, set_apart, 0, unroll=4)
    pl.semaphore_wait(barrier, 16)
    for n, (off, rows) in enumerate(((1, first), (3, second), (1, second), (3, first))):
        go(remote(wbuf.at[y, rows], wbuf.at[y, rows], wy_s.at[n], wy_r.at[n], c, peer(off)))
    for dz in along:
        pl.semaphore_signal(near_by, inc=1, device_id=(at(0, dz, 0), y), device_id_type=pl.DeviceIdType.MESH)
    acts_in.wait()

    def project(head, dest, lead):
        def tile(t, _):
            rows = pl.ds(t * 256, 256)
            total_ = jnp.dot(acts_v[rows, 0:1024], wbuf[head, 0:1024],
                             preferred_element_type=jnp.float32)
            for u in range(1, 4):
                total_ += jnp.dot(acts_v[rows, u * 1024:(u + 1) * 1024],
                                  wbuf[head, u * 1024:(u + 1) * 1024],
                                  preferred_element_type=jnp.float32)
            dest[pl.ds(lead + t * 2, 2)] = total_.astype(jnp.bfloat16).reshape(2, BLOCK, ROW)
            return 0
        lax.fori_loop(0, 2, tile, 0)

    project(y, kv, y * 4)

    offs = (1, 3, 2)

    def landed(view, send, recv):
        remote(view, view, send, recv, at(0, 0, 1), y).wait_recv()

    below, above = at(0, NZ - 1, 0), at(0, 1, 0)

    def in_plane(n):
        return at(n // 2, 0, n % 2)

    groups = {
        "own": (c, 0, 1, 8, in_plane),
        "below 3": (below, 7, 0, 4, lambda n: at(n, 3, 0)),
        "above 3": (above, 11, 0, 4, lambda n: at(n, NZ - 3, 1)),
        "below 2": (below, 15, 0, 8, lambda n: at(n // 2, 2, n % 2)),
        "above 2": (above, 23, 0, 8, lambda n: at(n // 2, NZ - 2, n % 2)),
        "below 1": (below, 31, 0, 8, lambda n: at(n // 2, 1, n % 2)),
        "above 1": (above, 39, 0, 8, lambda n: at(n // 2, NZ - 1, n % 2)),
        "below": (below, 47, 1, 8, in_plane),
        "above": (above, 54, 1, 8, in_plane),
    }
    keep = {"own": 61, "below": 62, "above": 63}

    def named_block(dst, source):
        found = jnp.int32(0)
        for r in range(RAND):
            for b in range(SHARD):
                v = rand[r * N_CTX * SHARD + dst * SHARD + b]
                found += jnp.where(v >> 4 == source, v & 15, 0)
        return found

    def look_up(name):
        source, base, lo, hi, dest_of = groups[name]

        def body(n, _):
            table[base + n - lo] = named_block(dest_of(n), source)
            return 0

        lax.fori_loop(lo, hi, body, 0)
        if name in keep:
            table[keep[name]] = named_block(c, source)

    def pick(name, buffer):
        source, base, lo, hi, dest_of = groups[name]
        if name in keep:
            pool[source] = buffer[table[keep[name]]]

        def body(n, _):
            slot = base + n - lo
            stage[slot] = buffer[table[slot]]
            remote(stage.at[slot], pool.at[source], st_s, pool_r, dest_of(n), y).start()
            return 0

        lax.fori_loop(lo, hi, body, 0)

    def multicast(n, head):
        rows = pl.ds(head * 4, 4)
        go(remote(kv.at[rows], before.at[rows], m_s.at[0, n], m_r.at[0, n], at(0, 1, 0), y))
        go(remote(kv.at[rows], after.at[rows], m_s.at[1, n], m_r.at[1, n], at(0, -1 + NZ, 0), y))

    def to_sibling(n, off):
        head = peer(off)
        go(remote(wbuf.at[head, whole], wbuf.at[head, whole], wd_s.at[0, n], wd_r.at[0, n],
                  at(0, 0, 1), y))

    def to_chips(n, off, part):
        head = peer(off)
        steps = ((1, 0), (NX - 1, 0), (0, 1), (0, NZ - 1))
        for j in (2 * part, 2 * part + 1):
            dx, dz = steps[j]
            rows = pl.ds(mine + j * SUB, SUB)
            go(remote(wbuf.at[head, rows], wbuf.at[head, rows], wx_s.at[n, j], wx_r.at[n, j],
                      at(dx, dz, 0), y))

    multicast(0, y)
    for name in groups:
        look_up(name)

    landed(wbuf.at[peer(3), first], wy_s.at[0], wy_r.at[0])
    go(remote(wbuf.at[peer(3), first], wbuf.at[peer(3), first], wy_s.at[4], wy_r.at[4], c, peer(1)))
    to_chips(1, 3, 0)
    landed(wbuf.at[peer(1), second], wy_s.at[1], wy_r.at[1])
    go(remote(wbuf.at[peer(1), second], wbuf.at[peer(1), second], wy_s.at[5], wy_r.at[5], c, peer(3)))
    to_chips(0, 1, 1)
    landed(wbuf.at[peer(3), second], wy_s.at[2], wy_r.at[2])
    to_chips(1, 3, 1)
    to_sibling(1, 3)
    landed(wbuf.at[peer(1), first], wy_s.at[3], wy_r.at[3])
    to_chips(0, 1, 0)
    to_sibling(0, 1)

    far = pl.ds(other, QUARTER)
    sib_mine = pl.ds((parity * 2 + 1 - k) * QUARTER, QUARTER)
    sib_other = pl.ds(((1 - parity) * 2 + 1 - k) * QUARTER, QUARTER)

    def pass_far(n, off):
        head = peer(off)
        for j in range(4):
            landed(wbuf.at[head, pl.ds(other + j * SUB, SUB)], wx_s.at[n, j], wx_r.at[n, j])
        go(remote(wbuf.at[head, far], wbuf.at[head, far], wd_s.at[1, n], wd_r.at[1, n],
                  at(0, 0, 1), y))

    def serve(n, off):
        head = peer(off)
        landed(wbuf.at[head, sib_mine], wd_s.at[0, n], wd_r.at[0, n])
        landed(wbuf.at[head, sib_other], wd_s.at[1, n], wd_r.at[1, n])
        project(head, kv_send.at[n], 0)
        go(remote(kv_send.at[n], kv.at[pl.ds(y * 4, 4)], kv_s.at[n], kv_r.at[n], c, head))

    pass_far(0, 1)
    pass_far(1, 3)
    landed(wbuf.at[peer(2), first], wy_s.at[4], wy_r.at[4])
    to_chips(2, 2, 0)
    landed(wbuf.at[peer(2), second], wy_s.at[5], wy_r.at[5])
    to_chips(2, 2, 1)
    to_sibling(2, 2)
    serve(0, 1)
    serve(1, 3)
    pass_far(2, 2)
    serve(2, 2)

    to_glob = pltpu.make_async_copy(kv.at[pl.ds(0, 2)], glob, loc.at[4])

    def root_copies():
        return [remote(kv.at[pl.ds(0, 2)], glob, g_s.at[n], g_r, at(0, dz, 0), y)
                for n, dz in enumerate((2, NZ - 2, 1, NZ - 1))]

    def up_copies():
        return [remote(glob, glob, g_s.at[4 + n], g_r, at(0, dz, 0), y) for n, dz in enumerate((2, 1))]

    def down_copies():
        return [remote(glob, glob, g_s.at[6], g_r, at(0, NZ - 1, 0), y)]

    def plane_copies():
        return [remote(glob, glob, g_s.at[6 + j], g_r, at(j // 2, 0, j % 2), y) for j in range(1, 8)]

    on_line = jnp.logical_and(x == 0, k == 0)
    tree = (
        (jnp.logical_and(on_line, z == 2), up_copies),
        (jnp.logical_and(on_line, z == NZ - 2), down_copies),
        (on_line, plane_copies),
    )

    def send_globals(holder):
        @pl.when(jnp.logical_and(c == 0, holder == 0))
        def _():
            for copy in root_copies():
                copy.start()
            to_glob.start()

    send_globals(y)

    for n, off in enumerate(offs):
        head = peer(NY - off)
        landed(kv.at[pl.ds(head * 4, 4)], kv_s.at[n], kv_r.at[n])
        send_globals(head)
        multicast(n + 1, head)

    @pl.when(c == 0)
    def _():
        to_glob.wait()

    @pl.when(jnp.logical_and(on_line, c != 0))
    def _():
        landed(glob, g_s.at[0], g_r)

    for holds, copies in tree:
        @pl.when(holds)
        def _():
            for copy in copies():
                copy.start()

    go(remote(kv.at[SHARD - 1], kvw.at[0], halo_s.at[0], halo_r.at[0], (c + 1) % N_CTX, y))
    go(remote(kv.at[0], kvw.at[SHARD + 1], halo_s.at[1], halo_r.at[1], (c + N_CTX - 1) % N_CTX, y))
    to_window = pltpu.make_async_copy(kv, kvw.at[pl.ds(1, SHARD)], loc.at[3])
    to_window.start()
    for n, off in enumerate(offs):
        head = peer(off)
        go(remote(queries.at[:, pl.ds(pl.multiple_of(head * QCOL, QCOL), QCOL)],
                  qx.at[pl.ds(y * TOK, TOK)], q_s.at[n], q_r.at[n], c, head))

    pick("own", kv)
    for n, off in enumerate((0, *offs)):
        rows = pl.ds(peer(NY - off) * 4, 4)
        landed(before.at[rows], m_s.at[0, n], m_r.at[0, n])
        landed(after.at[rows], m_s.at[1, n], m_r.at[1, n])
    pl.semaphore_wait(near_by, len(along))
    for name in groups:
        if name != "own":
            pick(name, before if name.startswith("below") else after)

    @pl.when(jnp.logical_not(on_line))
    def _():
        landed(glob, g_s.at[0], g_r)

    to_window.wait()
    landed(kvw.at[0], halo_s.at[0], halo_r.at[0])
    landed(kvw.at[SHARD + 1], halo_s.at[1], halo_r.at[1])
    own_q.wait()
    for n, off in enumerate(offs):
        landed(qx.at[pl.ds(peer(NY - off) * TOK, TOK)], q_s.at[n], q_r.at[n])

    half = GROUP // 2

    def stacked(i, part):
        rows = pl.ds(i * BLOCK, BLOCK)
        return jnp.concatenate(
            [qx[rows, g * HEAD:(g + 1) * HEAD] for g in range(part * half, (part + 1) * half)], axis=0
        )

    def near(i, _):
        keys = jnp.concatenate(
            [kvw[pl.ds(i, 3), :, 0:HEAD].reshape(3 * BLOCK, HEAD),
             glob[:, :, 0:HEAD].reshape(2 * BLOCK, HEAD)], axis=0)
        values = jnp.concatenate(
            [kvw[pl.ds(i, 3), :, HEAD:ROW].reshape(3 * BLOCK, HEAD),
             glob[:, :, HEAD:ROW].reshape(2 * BLOCK, HEAD)], axis=0)
        for part in range(2):
            rows = slice(part * half * BLOCK, (part + 1) * half * BLOCK)
            scores = lax.dot_general(stacked(i, part), keys, NT, preferred_element_type=jnp.float32)
            largest = jnp.max(scores, axis=-1, keepdims=True)
            weights = jnp.exp2((scores - largest) * EXP2_SCALE)
            top[i, rows] = largest
            total[i, rows] = jnp.sum(weights, axis=-1, keepdims=True)
            acc[i, rows] = jnp.dot(weights.astype(jnp.bfloat16), values,
                                   preferred_element_type=jnp.float32)
        return 0

    lax.fori_loop(0, SHARD, near, 0)

    landed(pool.at[pl.ds(0, SLOTS)], st_s, pool_r)

    def out_copy(j, i):
        column = pl.ds(pl.multiple_of(y * QCOL, QCOL), QCOL)
        return remote(outbox.at[pl.ds(i * BLOCK, BLOCK)],
                      out.at[pl.ds((i % 4) * BLOCK, BLOCK), column],
                      out_s.at[j], out_r.at[j], c, i // 4)

    def out_local(j, i):
        column = pl.ds(pl.multiple_of(y * QCOL, QCOL), QCOL)
        return pltpu.make_async_copy(outbox.at[pl.ds(i * BLOCK, BLOCK)],
                                     out.at[pl.ds((i % 4) * BLOCK, BLOCK), column], out_s.at[j])

    def block_of(j):
        step = j // 4
        off = jnp.where(step < 2, 2 - step, (3 - step) * 3)
        return ((y + off) % NY) * 4 + j % 4

    def finish(j, _):
        i = block_of(j)
        chosen = [pool[rand[r * N_CTX * SHARD + c * SHARD + i] >> 4] for r in range(RAND)]
        keys = jnp.concatenate([b[:, 0:HEAD] for b in chosen], axis=0)
        values = jnp.concatenate([b[:, HEAD:ROW] for b in chosen], axis=0)
        for part in range(2):
            rows = slice(part * half * BLOCK, (part + 1) * half * BLOCK)
            scores = lax.dot_general(stacked(i, part), keys, NT, preferred_element_type=jnp.float32)
            early = top[i, rows]
            largest = jnp.maximum(early, jnp.max(scores, axis=-1, keepdims=True))
            weights = jnp.exp2((scores - largest) * EXP2_SCALE)
            fade = jnp.exp2((early - largest) * EXP2_SCALE)
            mass = total[i, rows] * fade + jnp.sum(weights, axis=-1, keepdims=True)
            mixed = acc[i, rows] * fade + jnp.dot(weights.astype(jnp.bfloat16), values,
                                                  preferred_element_type=jnp.float32)
            result = (mixed / mass).astype(jnp.bfloat16)
            for g in range(half):
                column = (part * half + g) * HEAD
                outbox[pl.ds(i * BLOCK, BLOCK), column:column + HEAD] = result[g * BLOCK:(g + 1) * BLOCK]

        @pl.when(j < 12)
        def _():
            out_copy(j, i).start()

        @pl.when(j >= 12)
        def _():
            out_local(j, i).start()
        return 0

    lax.fori_loop(0, 16, finish, 0)

    for copy in sends:
        copy.wait_send()

    for holds, copies in ((c == 0, root_copies), *tree):
        @pl.when(holds)
        def _():
            for copy in copies():
                copy.wait_send()

    everything = stage.at[pl.ds(0, SLOTS)]
    remote(everything, pool.at[pl.ds(0, SLOTS)], st_s, pool_r, at(0, 0, 1), y).wait_send()

    def drain(j, _):
        i = block_of(j)

        @pl.when(j < 12)
        def _():
            out_copy(j, i).wait()

        @pl.when(j >= 12)
        def _():
            out_local(j, i).wait()
        return 0

    lax.fori_loop(0, 16, drain, 0)


def shards(acts, queries, kv_weight, rand_blocks):
    flat_weight = kv_weight.reshape(2 * MODEL, HEAD)
    bf16, f32 = jnp.bfloat16, jnp.float32
    blocks = pltpu.VMEM((SHARD, BLOCK, ROW), bf16)
    dma = pltpu.SemaphoreType.DMA
    return pl.pallas_call(
        kernel,
        out_shape=jax.ShapeDtypeStruct((TOK, NY * QCOL), bf16),
        in_specs=[pl.BlockSpec(memory_space=pltpu.SMEM)] + [pl.BlockSpec(memory_space=pl.ANY)] * 3,
        out_specs=pl.BlockSpec(memory_space=pl.ANY),
        scratch_shapes=[
            pltpu.VMEM((TOK, MODEL), bf16),
            pltpu.VMEM((NY, MODEL, ROW), bf16),
            pltpu.VMEM((3, 4, BLOCK, ROW), bf16),
            blocks,
            pltpu.VMEM((SHARD + 2, BLOCK, ROW), bf16),
            pltpu.VMEM((2, BLOCK, ROW), bf16),
            blocks, blocks,
            pltpu.VMEM((SLOTS, BLOCK, ROW), bf16),
            pltpu.VMEM((N_CTX, BLOCK, ROW), bf16),
            pltpu.VMEM((NY * TOK, QCOL), bf16),
            pltpu.VMEM((SHARD, GROUP * BLOCK, HEAD), f32),
            pltpu.VMEM((SHARD, GROUP * BLOCK, 1), f32),
            pltpu.VMEM((SHARD, GROUP * BLOCK, 1), f32),
            pltpu.VMEM((NY * TOK, QCOL), bf16),
            pltpu.SMEM((N_CTX,), jnp.int32),
            pltpu.VMEM((2 * MODEL, HEAD), bf16),
            dma((5,)), dma((6,)), dma((6,)), dma((2, 3)), dma((2, 3)), dma((3, 4)), dma((3, 4)),
            dma((3,)), dma((3,)), dma((3,)), dma((3,)),
            dma((2, 4)), dma((2, 4)), dma, dma, dma((2,)), dma((2,)), dma((14,)), dma,
            dma((16,)), dma((16,)), pltpu.SemaphoreType.REGULAR,
        ],
        compiler_params=pltpu.CompilerParams(
            collective_id=0, has_side_effects=True, vmem_limit_bytes=60 * 1024 * 1024
        ),
        cost_estimate=pl.CostEstimate(
            flops=9 * 10**9, bytes_accessed=12 * 2**20, transcendentals=8 * 2**20
        ),
    )(rand_blocks.T.reshape(-1), acts, queries, flat_weight)


def solution(mesh):
    placed = (P(("ctx", "fsdp"), None), P(("ctx", "fsdp"), None), P(None, "fsdp", None, None), P())
    return jax.shard_map(
        shards, mesh=mesh, in_specs=placed, out_specs=P(("ctx", "fsdp"), None), check_vma=False
    )
```

```python
import math

import jax
import jax.numpy as jnp
from jax import lax
from jax.experimental import pallas as pl
from jax.experimental.pallas import tpu as pltpu
from jax.sharding import PartitionSpec as P

BLOCK = 128
RAND = 3
NX, NZ, NY = 4, 8, 4
N_CTX = NX * NZ * 2
SHARD = 16
HEAD = 128
MODEL = 4096
TOK = 512
GROUP = 4
ROW = 2 * HEAD
QCOL = GROUP * HEAD
QUARTER = MODEL // 4
SUB = QUARTER // 4
SLOTS = 61
EXP2_SCALE = math.log2(math.e) / math.sqrt(HEAD)
NT = (((1,), (1,)), ((), ()))


def kernel(
    listed, acts, queries, weight, out,
    acts_v, wbuf, kv_send, kv, kvw, glob, before, after,
    stage, pool, qx, acc, top, total, outbox, table, pairs, rand,
    loc, wy_s, wy_r, wd_s, wd_r, wx_s, wx_r, kv_s, kv_r, q_s, q_r,
    m_s, m_r, st_s, pool_r, halo_s, halo_r, g_s, g_r, out_s, out_r, near_by,
):
    c = lax.axis_index("ctx")
    y = lax.axis_index("fsdp")
    x = c // (2 * NZ)
    z = (c // 2) % NZ
    k = c % 2
    parity = (x + z) % 2

    def at(dx, dz, dk):
        return (((x + dx) % NX) * NZ + (z + dz) % NZ) * 2 + (k + dk) % 2

    def remote(src, dst, send, recv, ctx, head):
        return pltpu.make_async_remote_copy(
            src_ref=src, dst_ref=dst, send_sem=send, recv_sem=recv,
            device_id=(ctx, head), device_id_type=pl.DeviceIdType.MESH,
        )

    def peer(off):
        return (y + off) % NY

    sends = []

    def go(copy):
        copy.start()
        sends.append(copy)

    mine = (parity * 2 + k) * QUARTER
    other = ((1 - parity) * 2 + k) * QUARTER
    whole = pl.ds(mine, QUARTER)
    first = pl.ds(mine, QUARTER // 2)
    second = pl.ds(mine + QUARTER // 2, QUARTER // 2)
    barrier = pltpu.get_barrier_semaphore()

    def greet(ctx, head):
        pl.semaphore_signal(barrier, inc=1, device_id=(ctx, head), device_id_type=pl.DeviceIdType.MESH)

    for off in range(1, NY):
        greet(c, peer(off))
    along = (1, NZ - 1, 2, NZ - 2, 3, NZ - 3)
    for dz in along:
        greet(at(0, dz, 0), y)
    for n in range(1, 8):
        greet(at(n // 2, 0, n % 2), y)
    named = pltpu.make_async_copy(listed, rand, loc.at[3])
    named.start()
    own_w = pltpu.make_async_copy(weight, pairs, loc.at[1])
    own_w.start()
    own_q = pltpu.make_async_copy(
        queries.at[:, pl.ds(pl.multiple_of(y * QCOL, QCOL), QCOL)],
        qx.at[pl.ds(y * TOK, TOK)], loc.at[2],
    )
    acts_in = pltpu.make_async_copy(acts, acts_v, loc.at[0])
    acts_in.start()
    own_q.start()
    own_w.wait()

    line = lax.broadcasted_iota(jnp.int32, (2 * BLOCK, 2 * BLOCK), 0)
    place = lax.broadcasted_iota(jnp.int32, (2 * BLOCK, 2 * BLOCK), 1)
    wanted = jnp.where(line < BLOCK, 2 * line, 2 * (line - BLOCK) + 1)
    order = jnp.where(place == wanted, 1.0, 0.0).astype(jnp.bfloat16)

    def set_apart(b, _):
        parts = jnp.dot(order, pairs[pl.ds(b * ROW, ROW)], preferred_element_type=jnp.float32)
        parts = parts.astype(jnp.bfloat16)
        rows = pl.ds(b * BLOCK, BLOCK)
        wbuf[y, rows, 0:HEAD] = parts[0:BLOCK]
        wbuf[y, rows, HEAD:ROW] = parts[BLOCK:2 * BLOCK]
        return 0

    lax.fori_loop(0, MODEL // BLOCK, set_apart, 0, unroll=4)
    pl.semaphore_wait(barrier, 16)
    for n, (off, rows) in enumerate(((1, first), (3, second), (1, second), (3, first))):
        go(remote(wbuf.at[y, rows], wbuf.at[y, rows], wy_s.at[n], wy_r.at[n], c, peer(off)))
    for dz in along:
        pl.semaphore_signal(near_by, inc=1, device_id=(at(0, dz, 0), y), device_id_type=pl.DeviceIdType.MESH)
    acts_in.wait()
    named.wait()

    def project(head, dest, lead):
        def tile(t, _):
            rows = pl.ds(t * 256, 256)
            total_ = jnp.dot(acts_v[rows, 0:1024], wbuf[head, 0:1024],
                             preferred_element_type=jnp.float32)
            for u in range(1, 4):
                total_ += jnp.dot(acts_v[rows, u * 1024:(u + 1) * 1024],
                                  wbuf[head, u * 1024:(u + 1) * 1024],
                                  preferred_element_type=jnp.float32)
            dest[pl.ds(lead + t * 2, 2)] = total_.astype(jnp.bfloat16).reshape(2, BLOCK, ROW)
            return 0
        lax.fori_loop(0, 2, tile, 0)

    project(y, kv, y * 4)

    offs = (1, 3, 2)

    def landed(view, send, recv):
        remote(view, view, send, recv, at(0, 0, 1), y).wait_recv()

    below, above = at(0, NZ - 1, 0), at(0, 1, 0)

    def in_plane(n):
        return at(n // 2, 0, n % 2)

    groups = {
        "own": (c, 0, 1, 8, in_plane),
        "below 3": (below, 7, 0, 4, lambda n: at(n, 3, 0)),
        "above 3": (above, 11, 0, 4, lambda n: at(n, NZ - 3, 1)),
        "below 2": (below, 15, 0, 8, lambda n: at(n // 2, 2, n % 2)),
        "above 2": (above, 23, 0, 8, lambda n: at(n // 2, NZ - 2, n % 2)),
        "below 1": (below, 31, 0, 8, lambda n: at(n // 2, 1, n % 2)),
        "above 1": (above, 39, 0, 8, lambda n: at(n // 2, NZ - 1, n % 2)),
        "below": (below, 47, 1, 8, in_plane),
        "above": (above, 54, 1, 8, in_plane),
    }
    keep = {"own": 61, "below": 62, "above": 63}

    def named_block(dst, source):
        found = jnp.int32(0)
        for r in range(RAND):
            for b in range(SHARD):
                v = rand[r, dst * SHARD + b]
                found += jnp.where(v >> 4 == source, v & 15, 0)
        return found

    def look_up(name):
        source, base, lo, hi, dest_of = groups[name]

        def body(n, _):
            table[base + n - lo] = named_block(dest_of(n), source)
            return 0

        lax.fori_loop(lo, hi, body, 0)
        if name in keep:
            table[keep[name]] = named_block(c, source)

    def pick(name, buffer):
        source, base, lo, hi, dest_of = groups[name]
        if name in keep:
            pool[source] = buffer[table[keep[name]]]

        def body(n, _):
            slot = base + n - lo
            stage[slot] = buffer[table[slot]]
            remote(stage.at[slot], pool.at[source], st_s, pool_r, dest_of(n), y).start()
            return 0

        lax.fori_loop(lo, hi, body, 0)

    def multicast(n, head):
        rows = pl.ds(head * 4, 4)
        go(remote(kv.at[rows], before.at[rows], m_s.at[0, n], m_r.at[0, n], at(0, 1, 0), y))
        go(remote(kv.at[rows], after.at[rows], m_s.at[1, n], m_r.at[1, n], at(0, -1 + NZ, 0), y))

    def to_sibling(n, off):
        head = peer(off)
        go(remote(wbuf.at[head, whole], wbuf.at[head, whole], wd_s.at[0, n], wd_r.at[0, n],
                  at(0, 0, 1), y))

    def to_chips(n, off, part):
        head = peer(off)
        steps = ((1, 0), (NX - 1, 0), (0, 1), (0, NZ - 1))
        for j in (2 * part, 2 * part + 1):
            dx, dz = steps[j]
            rows = pl.ds(mine + j * SUB, SUB)
            go(remote(wbuf.at[head, rows], wbuf.at[head, rows], wx_s.at[n, j], wx_r.at[n, j],
                      at(dx, dz, 0), y))

    multicast(0, y)
    for name in groups:
        look_up(name)

    landed(wbuf.at[peer(3), first], wy_s.at[0], wy_r.at[0])
    go(remote(wbuf.at[peer(3), first], wbuf.at[peer(3), first], wy_s.at[4], wy_r.at[4], c, peer(1)))
    to_chips(1, 3, 0)
    landed(wbuf.at[peer(1), second], wy_s.at[1], wy_r.at[1])
    go(remote(wbuf.at[peer(1), second], wbuf.at[peer(1), second], wy_s.at[5], wy_r.at[5], c, peer(3)))
    to_chips(0, 1, 1)
    landed(wbuf.at[peer(3), second], wy_s.at[2], wy_r.at[2])
    to_chips(1, 3, 1)
    to_sibling(1, 3)
    landed(wbuf.at[peer(1), first], wy_s.at[3], wy_r.at[3])
    to_chips(0, 1, 0)
    to_sibling(0, 1)

    far = pl.ds(other, QUARTER)
    sib_mine = pl.ds((parity * 2 + 1 - k) * QUARTER, QUARTER)
    sib_other = pl.ds(((1 - parity) * 2 + 1 - k) * QUARTER, QUARTER)

    def pass_far(n, off):
        head = peer(off)
        for j in range(4):
            landed(wbuf.at[head, pl.ds(other + j * SUB, SUB)], wx_s.at[n, j], wx_r.at[n, j])
        go(remote(wbuf.at[head, far], wbuf.at[head, far], wd_s.at[1, n], wd_r.at[1, n],
                  at(0, 0, 1), y))

    def serve(n, off):
        head = peer(off)
        landed(wbuf.at[head, sib_mine], wd_s.at[0, n], wd_r.at[0, n])
        landed(wbuf.at[head, sib_other], wd_s.at[1, n], wd_r.at[1, n])
        project(head, kv_send.at[n], 0)
        go(remote(kv_send.at[n], kv.at[pl.ds(y * 4, 4)], kv_s.at[n], kv_r.at[n], c, head))

    pass_far(0, 1)
    pass_far(1, 3)
    landed(wbuf.at[peer(2), first], wy_s.at[4], wy_r.at[4])
    to_chips(2, 2, 0)
    landed(wbuf.at[peer(2), second], wy_s.at[5], wy_r.at[5])
    to_chips(2, 2, 1)
    to_sibling(2, 2)
    serve(0, 1)
    serve(1, 3)
    pass_far(2, 2)
    serve(2, 2)

    to_glob = pltpu.make_async_copy(kv.at[pl.ds(0, 2)], glob, loc.at[4])

    def root_copies():
        return [remote(kv.at[pl.ds(0, 2)], glob, g_s.at[n], g_r, at(0, dz, 0), y)
                for n, dz in enumerate((2, NZ - 2, 1, NZ - 1))]

    def up_copies():
        return [remote(glob, glob, g_s.at[4 + n], g_r, at(0, dz, 0), y) for n, dz in enumerate((2, 1))]

    def down_copies():
        return [remote(glob, glob, g_s.at[6], g_r, at(0, NZ - 1, 0), y)]

    def plane_copies():
        return [remote(glob, glob, g_s.at[6 + j], g_r, at(j // 2, 0, j % 2), y) for j in range(1, 8)]

    on_line = jnp.logical_and(x == 0, k == 0)
    tree = (
        (jnp.logical_and(on_line, z == 2), up_copies),
        (jnp.logical_and(on_line, z == NZ - 2), down_copies),
        (on_line, plane_copies),
    )

    def send_globals(holder):
        @pl.when(jnp.logical_and(c == 0, holder == 0))
        def _():
            for copy in root_copies():
                copy.start()
            to_glob.start()

    send_globals(y)

    for n, off in enumerate(offs):
        head = peer(NY - off)
        landed(kv.at[pl.ds(head * 4, 4)], kv_s.at[n], kv_r.at[n])
        send_globals(head)
        multicast(n + 1, head)

    go(remote(kv.at[SHARD - 1], kvw.at[0], halo_s.at[0], halo_r.at[0], (c + 1) % N_CTX, y))
    go(remote(kv.at[0], kvw.at[SHARD + 1], halo_s.at[1], halo_r.at[1], (c + N_CTX - 1) % N_CTX, y))
    to_window = pltpu.make_async_copy(kv, kvw.at[pl.ds(1, SHARD)], loc.at[3])
    to_window.start()
    for n, off in enumerate(offs):
        head = peer(off)
        go(remote(queries.at[:, pl.ds(pl.multiple_of(head * QCOL, QCOL), QCOL)],
                  qx.at[pl.ds(y * TOK, TOK)], q_s.at[n], q_r.at[n], c, head))

    pick("own", kv)

    @pl.when(c == 0)
    def _():
        to_glob.wait()

    @pl.when(jnp.logical_and(on_line, c != 0))
    def _():
        landed(glob, g_s.at[0], g_r)

    for holds, copies in tree:
        @pl.when(holds)
        def _():
            for copy in copies():
                copy.start()

    for n, off in enumerate((0, *offs)):
        rows = pl.ds(peer(NY - off) * 4, 4)
        landed(before.at[rows], m_s.at[0, n], m_r.at[0, n])
        landed(after.at[rows], m_s.at[1, n], m_r.at[1, n])
    pl.semaphore_wait(near_by, len(along))
    for name in groups:
        if name != "own":
            pick(name, before if name.startswith("below") else after)

    @pl.when(jnp.logical_not(on_line))
    def _():
        landed(glob, g_s.at[0], g_r)

    to_window.wait()
    landed(kvw.at[0], halo_s.at[0], halo_r.at[0])
    landed(kvw.at[SHARD + 1], halo_s.at[1], halo_r.at[1])
    own_q.wait()
    for n, off in enumerate(offs):
        landed(qx.at[pl.ds(peer(NY - off) * TOK, TOK)], q_s.at[n], q_r.at[n])

    half = GROUP // 2

    def stacked(i, part):
        rows = pl.ds(i * BLOCK, BLOCK)
        return jnp.concatenate(
            [qx[rows, g * HEAD:(g + 1) * HEAD] for g in range(part * half, (part + 1) * half)], axis=0
        )

    def near(i, _):
        keys = jnp.concatenate(
            [kvw[pl.ds(i, 3), :, 0:HEAD].reshape(3 * BLOCK, HEAD),
             glob[:, :, 0:HEAD].reshape(2 * BLOCK, HEAD)], axis=0)
        values = jnp.concatenate(
            [kvw[pl.ds(i, 3), :, HEAD:ROW].reshape(3 * BLOCK, HEAD),
             glob[:, :, HEAD:ROW].reshape(2 * BLOCK, HEAD)], axis=0)
        for part in range(2):
            rows = slice(part * half * BLOCK, (part + 1) * half * BLOCK)
            scores = lax.dot_general(stacked(i, part), keys, NT, preferred_element_type=jnp.float32)
            largest = jnp.max(scores, axis=-1, keepdims=True)
            weights = jnp.exp2((scores - largest) * EXP2_SCALE)
            top[i, rows] = largest
            total[i, rows] = jnp.sum(weights, axis=-1, keepdims=True)
            acc[i, rows] = jnp.dot(weights.astype(jnp.bfloat16), values,
                                   preferred_element_type=jnp.float32)
        return 0

    lax.fori_loop(0, SHARD, near, 0)

    landed(pool.at[pl.ds(0, SLOTS)], st_s, pool_r)

    def out_copy(j, i):
        column = pl.ds(pl.multiple_of(y * QCOL, QCOL), QCOL)
        return remote(outbox.at[pl.ds(i * BLOCK, BLOCK)],
                      out.at[pl.ds((i % 4) * BLOCK, BLOCK), column],
                      out_s.at[j], out_r.at[j], c, i // 4)

    def out_local(j, i):
        column = pl.ds(pl.multiple_of(y * QCOL, QCOL), QCOL)
        return pltpu.make_async_copy(outbox.at[pl.ds(i * BLOCK, BLOCK)],
                                     out.at[pl.ds((i % 4) * BLOCK, BLOCK), column], out_s.at[j])

    def block_of(j):
        step = j // 4
        off = jnp.where(step < 2, 2 - step, (3 - step) * 3)
        return ((y + off) % NY) * 4 + j % 4

    def finish(j, _):
        i = block_of(j)
        chosen = [pool[rand[r, c * SHARD + i] >> 4] for r in range(RAND)]
        keys = jnp.concatenate([b[:, 0:HEAD] for b in chosen], axis=0)
        values = jnp.concatenate([b[:, HEAD:ROW] for b in chosen], axis=0)
        for part in range(2):
            rows = slice(part * half * BLOCK, (part + 1) * half * BLOCK)
            scores = lax.dot_general(stacked(i, part), keys, NT, preferred_element_type=jnp.float32)
            early = top[i, rows]
            largest = jnp.maximum(early, jnp.max(scores, axis=-1, keepdims=True))
            weights = jnp.exp2((scores - largest) * EXP2_SCALE)
            fade = jnp.exp2((early - largest) * EXP2_SCALE)
            mass = total[i, rows] * fade + jnp.sum(weights, axis=-1, keepdims=True)
            mixed = acc[i, rows] * fade + jnp.dot(weights.astype(jnp.bfloat16), values,
                                                  preferred_element_type=jnp.float32)
            result = (mixed / mass).astype(jnp.bfloat16)
            for g in range(half):
                column = (part * half + g) * HEAD
                outbox[pl.ds(i * BLOCK, BLOCK), column:column + HEAD] = result[g * BLOCK:(g + 1) * BLOCK]

        @pl.when(j < 12)
        def _():
            out_copy(j, i).start()

        @pl.when(j >= 12)
        def _():
            out_local(j, i).start()
        return 0

    lax.fori_loop(0, 16, finish, 0)

    for copy in sends:
        copy.wait_send()

    for holds, copies in ((c == 0, root_copies), *tree):
        @pl.when(holds)
        def _():
            for copy in copies():
                copy.wait_send()

    everything = stage.at[pl.ds(0, SLOTS)]
    remote(everything, pool.at[pl.ds(0, SLOTS)], st_s, pool_r, at(0, 0, 1), y).wait_send()

    def drain(j, _):
        i = block_of(j)

        @pl.when(j < 12)
        def _():
            out_copy(j, i).wait()

        @pl.when(j >= 12)
        def _():
            out_local(j, i).wait()
        return 0

    lax.fori_loop(0, 16, drain, 0)


def shards(acts, queries, kv_weight, rand_blocks):
    flat_weight = kv_weight.reshape(2 * MODEL, HEAD)
    bf16, f32 = jnp.bfloat16, jnp.float32
    blocks = pltpu.VMEM((SHARD, BLOCK, ROW), bf16)
    dma = pltpu.SemaphoreType.DMA
    attended = pl.pallas_call(
        kernel,
        out_shape=jax.ShapeDtypeStruct((TOK, NY * QCOL), bf16),
        in_specs=[pl.BlockSpec(memory_space=pl.ANY)] * 4,
        out_specs=pl.BlockSpec(memory_space=pl.ANY),
        scratch_shapes=[
            pltpu.VMEM((TOK, MODEL), bf16),
            pltpu.VMEM((NY, MODEL, ROW), bf16),
            pltpu.VMEM((3, 4, BLOCK, ROW), bf16),
            blocks,
            pltpu.VMEM((SHARD + 2, BLOCK, ROW), bf16),
            pltpu.VMEM((2, BLOCK, ROW), bf16),
            blocks, blocks,
            pltpu.VMEM((SLOTS, BLOCK, ROW), bf16),
            pltpu.VMEM((N_CTX, BLOCK, ROW), bf16),
            pltpu.VMEM((NY * TOK, QCOL), bf16),
            pltpu.VMEM((SHARD, GROUP * BLOCK, HEAD), f32),
            pltpu.VMEM((SHARD, GROUP * BLOCK, 1), f32),
            pltpu.VMEM((SHARD, GROUP * BLOCK, 1), f32),
            pltpu.VMEM((NY * TOK, QCOL), bf16),
            pltpu.SMEM((N_CTX,), jnp.int32),
            pltpu.VMEM((2 * MODEL, HEAD), bf16),
            pltpu.SMEM((RAND, N_CTX * SHARD), jnp.int32),
            dma((5,)), dma((6,)), dma((6,)), dma((2, 3)), dma((2, 3)), dma((3, 4)), dma((3, 4)),
            dma((3,)), dma((3,)), dma((3,)), dma((3,)),
            dma((2, 4)), dma((2, 4)), dma, dma, dma((2,)), dma((2,)), dma((14,)), dma,
            dma((16,)), dma((16,)), pltpu.SemaphoreType.REGULAR,
        ],
        compiler_params=pltpu.CompilerParams(
            collective_id=0, has_side_effects=True, vmem_limit_bytes=60 * 1024 * 1024
        ),
        cost_estimate=pl.CostEstimate(
            flops=9 * 10**9, bytes_accessed=12 * 2**20, transcendentals=8 * 2**20
        ),
    )(rand_blocks.T, acts, queries, flat_weight)
    parts = 8

    def hand_over(source, dest, held, came, left):
        rows = [pl.ds(n * TOK // parts, TOK // parts) for n in range(parts)]
        reads = [pltpu.make_async_copy(source.at[r], held.at[r], came.at[n]) for n, r in enumerate(rows)]
        writes = [pltpu.make_async_copy(held.at[r], dest.at[r], left.at[n]) for n, r in enumerate(rows)]
        for copy in reads:
            copy.start()
        for read, write in zip(reads, writes):
            read.wait()
            write.start()
        for copy in writes:
            copy.wait()

    return pl.pallas_call(
        hand_over,
        out_shape=jax.ShapeDtypeStruct((TOK, NY * QCOL), bf16),
        in_specs=[pl.BlockSpec(memory_space=pl.ANY)],
        out_specs=pl.BlockSpec(memory_space=pl.ANY),
        scratch_shapes=[pltpu.VMEM((TOK, NY * QCOL), bf16), dma((parts,)), dma((parts,))],
        compiler_params=pltpu.CompilerParams(vmem_limit_bytes=60 * 1024 * 1024),
    )(attended)


def solution(mesh):
    placed = (P(("ctx", "fsdp"), None), P(("ctx", "fsdp"), None), P(None, "fsdp", None, None), P())
    return jax.shard_map(
        shards, mesh=mesh, in_specs=placed, out_specs=P(("ctx", "fsdp"), None), check_vma=False
    )
```

```python
import math

import jax
import jax.numpy as jnp
from jax import lax
from jax.experimental import pallas as pl
from jax.experimental.pallas import tpu as pltpu
from jax.sharding import PartitionSpec as P

BLOCK = 128
RAND = 3
NX, NZ, NY = 4, 8, 4
N_CTX = NX * NZ * 2
SHARD = 16
HEAD = 128
MODEL = 4096
TOK = 512
GROUP = 4
ROW = 2 * HEAD
QCOL = GROUP * HEAD
QUARTER = MODEL // 4
SUB = QUARTER // 4
SLOTS = 61
EXP2_SCALE = math.log2(math.e) / math.sqrt(HEAD)
NT = (((1,), (1,)), ((), ()))


def kernel(
    listed, acts, queries, weight, out,
    acts_v, wbuf, kv_send, kv, kvw, glob, before, after,
    stage, pool, qx, acc, top, total, outbox, table, pairs, rand,
    loc, wy_s, wy_r, wd_s, wd_r, wx_s, wx_r, kv_s, kv_r, q_s, q_r,
    m_s, m_r, st_s, pool_r, halo_s, halo_r, g_s, g_r, out_s, out_r, near_by,
):
    c = lax.axis_index("ctx")
    y = lax.axis_index("fsdp")
    x = c // (2 * NZ)
    z = (c // 2) % NZ
    k = c % 2
    parity = (x + z) % 2

    def at(dx, dz, dk):
        return (((x + dx) % NX) * NZ + (z + dz) % NZ) * 2 + (k + dk) % 2

    def remote(src, dst, send, recv, ctx, head):
        return pltpu.make_async_remote_copy(
            src_ref=src, dst_ref=dst, send_sem=send, recv_sem=recv,
            device_id=(ctx, head), device_id_type=pl.DeviceIdType.MESH,
        )

    def peer(off):
        return (y + off) % NY

    sends = []

    def go(copy):
        copy.start()
        sends.append(copy)

    mine = (parity * 2 + k) * QUARTER
    other = ((1 - parity) * 2 + k) * QUARTER
    whole = pl.ds(mine, QUARTER)
    first = pl.ds(mine, QUARTER // 2)
    second = pl.ds(mine + QUARTER // 2, QUARTER // 2)
    barrier = pltpu.get_barrier_semaphore()

    def greet(ctx, head):
        pl.semaphore_signal(barrier, inc=1, device_id=(ctx, head), device_id_type=pl.DeviceIdType.MESH)

    for off in range(1, NY):
        greet(c, peer(off))
    along = (1, NZ - 1, 2, NZ - 2, 3, NZ - 3)
    for dz in along:
        greet(at(0, dz, 0), y)
    for n in range(1, 8):
        greet(at(n // 2, 0, n % 2), y)
    own_w = []
    for n, slot in enumerate((1, 5, 6, 7)):
        part = pl.ds((parity * 2 + k + n) % 4 * (2 * QUARTER), 2 * QUARTER)
        own_w.append(pltpu.make_async_copy(weight.at[part], pairs.at[part], loc.at[slot]))
        own_w[n].start()
    named = pltpu.make_async_copy(listed, rand, loc.at[3])
    named.start()
    own_q = pltpu.make_async_copy(
        queries.at[:, pl.ds(pl.multiple_of(y * QCOL, QCOL), QCOL)],
        qx.at[pl.ds(y * TOK, TOK)], loc.at[2],
    )
    acts_in = pltpu.make_async_copy(acts, acts_v, loc.at[0])
    acts_in.start()
    own_q.start()

    line = lax.broadcasted_iota(jnp.int32, (2 * BLOCK, 2 * BLOCK), 0)
    place = lax.broadcasted_iota(jnp.int32, (2 * BLOCK, 2 * BLOCK), 1)
    wanted = jnp.where(line < BLOCK, 2 * line, 2 * (line - BLOCK) + 1)
    order = jnp.where(place == wanted, 1.0, 0.0).astype(jnp.bfloat16)

    def set_apart(b, _):
        parts = jnp.dot(order, pairs[pl.ds(b * ROW, ROW)], preferred_element_type=jnp.float32)
        parts = parts.astype(jnp.bfloat16)
        rows = pl.ds(b * BLOCK, BLOCK)
        wbuf[y, rows, 0:HEAD] = parts[0:BLOCK]
        wbuf[y, rows, HEAD:ROW] = parts[BLOCK:2 * BLOCK]
        return 0

    def set_quarter_apart(n):
        own_w[n].wait()
        start = (parity * 2 + k + n) % 4 * (QUARTER // BLOCK)
        lax.fori_loop(0, QUARTER // BLOCK, lambda b, _: set_apart(start + b, 0), 0, unroll=4)

    set_quarter_apart(0)
    pl.semaphore_wait(barrier, 16)
    for n, (off, rows) in enumerate(((1, first), (3, second), (1, second), (3, first))):
        go(remote(wbuf.at[y, rows], wbuf.at[y, rows], wy_s.at[n], wy_r.at[n], c, peer(off)))
    for dz in along:
        pl.semaphore_signal(near_by, inc=1, device_id=(at(0, dz, 0), y), device_id_type=pl.DeviceIdType.MESH)
    for n in range(1, 4):
        set_quarter_apart(n)
    acts_in.wait()
    named.wait()

    def project(head, dest, lead):
        def tile(t, _):
            rows = pl.ds(t * 256, 256)
            total_ = jnp.dot(acts_v[rows, 0:1024], wbuf[head, 0:1024],
                             preferred_element_type=jnp.float32)
            for u in range(1, 4):
                total_ += jnp.dot(acts_v[rows, u * 1024:(u + 1) * 1024],
                                  wbuf[head, u * 1024:(u + 1) * 1024],
                                  preferred_element_type=jnp.float32)
            dest[pl.ds(lead + t * 2, 2)] = total_.astype(jnp.bfloat16).reshape(2, BLOCK, ROW)
            return 0
        lax.fori_loop(0, 2, tile, 0)

    project(y, kv, y * 4)

    offs = (1, 3, 2)

    def landed(view, send, recv):
        remote(view, view, send, recv, at(0, 0, 1), y).wait_recv()

    below, above = at(0, NZ - 1, 0), at(0, 1, 0)

    def in_plane(n):
        return at(n // 2, 0, n % 2)

    groups = {
        "own": (c, 0, 1, 8, in_plane),
        "below 3": (below, 7, 0, 4, lambda n: at(n, 3, 0)),
        "above 3": (above, 11, 0, 4, lambda n: at(n, NZ - 3, 1)),
        "below 2": (below, 15, 0, 8, lambda n: at(n // 2, 2, n % 2)),
        "above 2": (above, 23, 0, 8, lambda n: at(n // 2, NZ - 2, n % 2)),
        "below 1": (below, 31, 0, 8, lambda n: at(n // 2, 1, n % 2)),
        "above 1": (above, 39, 0, 8, lambda n: at(n // 2, NZ - 1, n % 2)),
        "below": (below, 47, 1, 8, in_plane),
        "above": (above, 54, 1, 8, in_plane),
    }
    keep = {"own": 61, "below": 62, "above": 63}

    def named_block(dst, source):
        found = jnp.int32(0)
        for r in range(RAND):
            for b in range(SHARD):
                v = rand[r, dst * SHARD + b]
                found += jnp.where(v >> 4 == source, v & 15, 0)
        return found

    def look_up(name):
        source, base, lo, hi, dest_of = groups[name]

        def body(n, _):
            table[base + n - lo] = named_block(dest_of(n), source)
            return 0

        lax.fori_loop(lo, hi, body, 0)
        if name in keep:
            table[keep[name]] = named_block(c, source)

    def pick(name, buffer):
        source, base, lo, hi, dest_of = groups[name]
        if name in keep:
            pool[source] = buffer[table[keep[name]]]

        def body(n, _):
            slot = base + n - lo
            stage[slot] = buffer[table[slot]]
            remote(stage.at[slot], pool.at[source], st_s, pool_r, dest_of(n), y).start()
            return 0

        lax.fori_loop(lo, hi, body, 0)

    def multicast(n, head):
        rows = pl.ds(head * 4, 4)
        go(remote(kv.at[rows], before.at[rows], m_s.at[0, n], m_r.at[0, n], at(0, 1, 0), y))
        go(remote(kv.at[rows], after.at[rows], m_s.at[1, n], m_r.at[1, n], at(0, -1 + NZ, 0), y))

    def to_sibling(n, off):
        head = peer(off)
        go(remote(wbuf.at[head, whole], wbuf.at[head, whole], wd_s.at[0, n], wd_r.at[0, n],
                  at(0, 0, 1), y))

    def to_chips(n, off, part):
        head = peer(off)
        steps = ((1, 0), (NX - 1, 0), (0, 1), (0, NZ - 1))
        for j in (2 * part, 2 * part + 1):
            dx, dz = steps[j]
            rows = pl.ds(mine + j * SUB, SUB)
            go(remote(wbuf.at[head, rows], wbuf.at[head, rows], wx_s.at[n, j], wx_r.at[n, j],
                      at(dx, dz, 0), y))

    multicast(0, y)
    for name in groups:
        look_up(name)

    landed(wbuf.at[peer(3), first], wy_s.at[0], wy_r.at[0])
    go(remote(wbuf.at[peer(3), first], wbuf.at[peer(3), first], wy_s.at[4], wy_r.at[4], c, peer(1)))
    to_chips(1, 3, 0)
    landed(wbuf.at[peer(1), second], wy_s.at[1], wy_r.at[1])
    go(remote(wbuf.at[peer(1), second], wbuf.at[peer(1), second], wy_s.at[5], wy_r.at[5], c, peer(3)))
    to_chips(0, 1, 1)
    landed(wbuf.at[peer(3), second], wy_s.at[2], wy_r.at[2])
    to_chips(1, 3, 1)
    to_sibling(1, 3)
    landed(wbuf.at[peer(1), first], wy_s.at[3], wy_r.at[3])
    to_chips(0, 1, 0)
    to_sibling(0, 1)

    far = pl.ds(other, QUARTER)
    sib_mine = pl.ds((parity * 2 + 1 - k) * QUARTER, QUARTER)
    sib_other = pl.ds(((1 - parity) * 2 + 1 - k) * QUARTER, QUARTER)

    def pass_far(n, off):
        head = peer(off)
        for j in range(4):
            landed(wbuf.at[head, pl.ds(other + j * SUB, SUB)], wx_s.at[n, j], wx_r.at[n, j])
        go(remote(wbuf.at[head, far], wbuf.at[head, far], wd_s.at[1, n], wd_r.at[1, n],
                  at(0, 0, 1), y))

    def serve(n, off):
        head = peer(off)
        landed(wbuf.at[head, sib_mine], wd_s.at[0, n], wd_r.at[0, n])
        landed(wbuf.at[head, sib_other], wd_s.at[1, n], wd_r.at[1, n])
        project(head, kv_send.at[n], 0)
        go(remote(kv_send.at[n], kv.at[pl.ds(y * 4, 4)], kv_s.at[n], kv_r.at[n], c, head))

    pass_far(0, 1)
    pass_far(1, 3)
    landed(wbuf.at[peer(2), first], wy_s.at[4], wy_r.at[4])
    to_chips(2, 2, 0)
    landed(wbuf.at[peer(2), second], wy_s.at[5], wy_r.at[5])
    to_chips(2, 2, 1)
    to_sibling(2, 2)
    serve(0, 1)
    serve(1, 3)
    pass_far(2, 2)
    serve(2, 2)

    to_glob = pltpu.make_async_copy(kv.at[pl.ds(0, 2)], glob, loc.at[4])

    def root_copies():
        return [remote(kv.at[pl.ds(0, 2)], glob, g_s.at[n], g_r, at(0, dz, 0), y)
                for n, dz in enumerate((2, NZ - 2, 1, NZ - 1))]

    def up_copies():
        return [remote(glob, glob, g_s.at[4 + n], g_r, at(0, dz, 0), y) for n, dz in enumerate((2, 1))]

    def down_copies():
        return [remote(glob, glob, g_s.at[6], g_r, at(0, NZ - 1, 0), y)]

    def plane_copies():
        return [remote(glob, glob, g_s.at[6 + j], g_r, at(j // 2, 0, j % 2), y) for j in range(1, 8)]

    on_line = jnp.logical_and(x == 0, k == 0)
    tree = (
        (jnp.logical_and(on_line, z == 2), up_copies),
        (jnp.logical_and(on_line, z == NZ - 2), down_copies),
        (on_line, plane_copies),
    )

    def send_globals(holder):
        @pl.when(jnp.logical_and(c == 0, holder == 0))
        def _():
            for copy in root_copies():
                copy.start()
            to_glob.start()

    send_globals(y)

    for n, off in enumerate(offs):
        head = peer(NY - off)
        landed(kv.at[pl.ds(head * 4, 4)], kv_s.at[n], kv_r.at[n])
        send_globals(head)
        multicast(n + 1, head)

    go(remote(kv.at[SHARD - 1], kvw.at[0], halo_s.at[0], halo_r.at[0], (c + 1) % N_CTX, y))
    go(remote(kv.at[0], kvw.at[SHARD + 1], halo_s.at[1], halo_r.at[1], (c + N_CTX - 1) % N_CTX, y))
    to_window = pltpu.make_async_copy(kv, kvw.at[pl.ds(1, SHARD)], loc.at[3])
    to_window.start()
    for n, off in enumerate(offs):
        head = peer(off)
        go(remote(queries.at[:, pl.ds(pl.multiple_of(head * QCOL, QCOL), QCOL)],
                  qx.at[pl.ds(y * TOK, TOK)], q_s.at[n], q_r.at[n], c, head))

    pick("own", kv)

    @pl.when(c == 0)
    def _():
        to_glob.wait()

    @pl.when(jnp.logical_and(on_line, c != 0))
    def _():
        landed(glob, g_s.at[0], g_r)

    for holds, copies in tree:
        @pl.when(holds)
        def _():
            for copy in copies():
                copy.start()

    for n, off in enumerate((0, *offs)):
        rows = pl.ds(peer(NY - off) * 4, 4)
        landed(before.at[rows], m_s.at[0, n], m_r.at[0, n])
        landed(after.at[rows], m_s.at[1, n], m_r.at[1, n])
    pl.semaphore_wait(near_by, len(along))
    for name in groups:
        if name != "own":
            pick(name, before if name.startswith("below") else after)

    @pl.when(jnp.logical_not(on_line))
    def _():
        landed(glob, g_s.at[0], g_r)

    to_window.wait()
    landed(kvw.at[0], halo_s.at[0], halo_r.at[0])
    landed(kvw.at[SHARD + 1], halo_s.at[1], halo_r.at[1])
    own_q.wait()
    for n, off in enumerate(offs):
        landed(qx.at[pl.ds(peer(NY - off) * TOK, TOK)], q_s.at[n], q_r.at[n])

    half = GROUP // 2

    def stacked(i, part):
        rows = pl.ds(i * BLOCK, BLOCK)
        return jnp.concatenate(
            [qx[rows, g * HEAD:(g + 1) * HEAD] for g in range(part * half, (part + 1) * half)], axis=0
        )

    def near(i, _):
        keys = jnp.concatenate(
            [kvw[pl.ds(i, 3), :, 0:HEAD].reshape(3 * BLOCK, HEAD),
             glob[:, :, 0:HEAD].reshape(2 * BLOCK, HEAD)], axis=0)
        values = jnp.concatenate(
            [kvw[pl.ds(i, 3), :, HEAD:ROW].reshape(3 * BLOCK, HEAD),
             glob[:, :, HEAD:ROW].reshape(2 * BLOCK, HEAD)], axis=0)
        for part in range(2):
            rows = slice(part * half * BLOCK, (part + 1) * half * BLOCK)
            scores = lax.dot_general(stacked(i, part), keys, NT, preferred_element_type=jnp.float32)
            largest = jnp.max(scores, axis=-1, keepdims=True)
            weights = jnp.exp2((scores - largest) * EXP2_SCALE)
            top[i, rows] = largest
            total[i, rows] = jnp.sum(weights, axis=-1, keepdims=True)
            acc[i, rows] = jnp.dot(weights.astype(jnp.bfloat16), values,
                                   preferred_element_type=jnp.float32)
        return 0

    lax.fori_loop(0, SHARD, near, 0)

    landed(pool.at[pl.ds(0, SLOTS)], st_s, pool_r)

    def out_copy(j, i):
        column = pl.ds(pl.multiple_of(y * QCOL, QCOL), QCOL)
        return remote(outbox.at[pl.ds(i * BLOCK, BLOCK)],
                      out.at[pl.ds((i % 4) * BLOCK, BLOCK), column],
                      out_s.at[j], out_r.at[j], c, i // 4)

    def out_local(j, i):
        column = pl.ds(pl.multiple_of(y * QCOL, QCOL), QCOL)
        return pltpu.make_async_copy(outbox.at[pl.ds(i * BLOCK, BLOCK)],
                                     out.at[pl.ds((i % 4) * BLOCK, BLOCK), column], out_s.at[j])

    def block_of(j):
        step = j // 4
        off = jnp.where(step < 2, 2 - step, (3 - step) * 3)
        return ((y + off) % NY) * 4 + j % 4

    def finish(j, _):
        i = block_of(j)
        chosen = [pool[rand[r, c * SHARD + i] >> 4] for r in range(RAND)]
        keys = jnp.concatenate([b[:, 0:HEAD] for b in chosen], axis=0)
        values = jnp.concatenate([b[:, HEAD:ROW] for b in chosen], axis=0)
        for part in range(2):
            rows = slice(part * half * BLOCK, (part + 1) * half * BLOCK)
            scores = lax.dot_general(stacked(i, part), keys, NT, preferred_element_type=jnp.float32)
            early = top[i, rows]
            largest = jnp.maximum(early, jnp.max(scores, axis=-1, keepdims=True))
            weights = jnp.exp2((scores - largest) * EXP2_SCALE)
            fade = jnp.exp2((early - largest) * EXP2_SCALE)
            mass = total[i, rows] * fade + jnp.sum(weights, axis=-1, keepdims=True)
            mixed = acc[i, rows] * fade + jnp.dot(weights.astype(jnp.bfloat16), values,
                                                  preferred_element_type=jnp.float32)
            result = (mixed / mass).astype(jnp.bfloat16)
            for g in range(half):
                column = (part * half + g) * HEAD
                outbox[pl.ds(i * BLOCK, BLOCK), column:column + HEAD] = result[g * BLOCK:(g + 1) * BLOCK]

        @pl.when(j < 12)
        def _():
            out_copy(j, i).start()

        @pl.when(j >= 12)
        def _():
            out_local(j, i).start()
        return 0

    lax.fori_loop(0, 16, finish, 0)

    for copy in sends:
        copy.wait_send()

    for holds, copies in ((c == 0, root_copies), *tree):
        @pl.when(holds)
        def _():
            for copy in copies():
                copy.wait_send()

    everything = stage.at[pl.ds(0, SLOTS)]
    remote(everything, pool.at[pl.ds(0, SLOTS)], st_s, pool_r, at(0, 0, 1), y).wait_send()

    def drain(j, _):
        i = block_of(j)

        @pl.when(j < 12)
        def _():
            out_copy(j, i).wait()

        @pl.when(j >= 12)
        def _():
            out_local(j, i).wait()
        return 0

    lax.fori_loop(0, 16, drain, 0)


def shards(acts, queries, kv_weight, rand_blocks):
    flat_weight = kv_weight.reshape(2 * MODEL, HEAD)
    bf16, f32 = jnp.bfloat16, jnp.float32
    blocks = pltpu.VMEM((SHARD, BLOCK, ROW), bf16)
    dma = pltpu.SemaphoreType.DMA
    attended = pl.pallas_call(
        kernel,
        out_shape=jax.ShapeDtypeStruct((TOK, NY * QCOL), bf16),
        in_specs=[pl.BlockSpec(memory_space=pl.ANY)] * 4,
        out_specs=pl.BlockSpec(memory_space=pl.ANY),
        scratch_shapes=[
            pltpu.VMEM((TOK, MODEL), bf16),
            pltpu.VMEM((NY, MODEL, ROW), bf16),
            pltpu.VMEM((3, 4, BLOCK, ROW), bf16),
            blocks,
            pltpu.VMEM((SHARD + 2, BLOCK, ROW), bf16),
            pltpu.VMEM((2, BLOCK, ROW), bf16),
            blocks, blocks,
            pltpu.VMEM((SLOTS, BLOCK, ROW), bf16),
            pltpu.VMEM((N_CTX, BLOCK, ROW), bf16),
            pltpu.VMEM((NY * TOK, QCOL), bf16),
            pltpu.VMEM((SHARD, GROUP * BLOCK, HEAD), f32),
            pltpu.VMEM((SHARD, GROUP * BLOCK, 1), f32),
            pltpu.VMEM((SHARD, GROUP * BLOCK, 1), f32),
            pltpu.VMEM((NY * TOK, QCOL), bf16),
            pltpu.SMEM((N_CTX,), jnp.int32),
            pltpu.VMEM((2 * MODEL, HEAD), bf16),
            pltpu.SMEM((RAND, N_CTX * SHARD), jnp.int32),
            dma((8,)), dma((6,)), dma((6,)), dma((2, 3)), dma((2, 3)), dma((3, 4)), dma((3, 4)),
            dma((3,)), dma((3,)), dma((3,)), dma((3,)),
            dma((2, 4)), dma((2, 4)), dma, dma, dma((2,)), dma((2,)), dma((14,)), dma,
            dma((16,)), dma((16,)), pltpu.SemaphoreType.REGULAR,
        ],
        compiler_params=pltpu.CompilerParams(
            collective_id=0, has_side_effects=True, vmem_limit_bytes=60 * 1024 * 1024
        ),
        cost_estimate=pl.CostEstimate(
            flops=9 * 10**9, bytes_accessed=12 * 2**20, transcendentals=8 * 2**20
        ),
    )(rand_blocks.T, acts, queries, flat_weight)
    parts = 8

    def hand_over(source, dest, held, came, left):
        rows = [pl.ds(n * TOK // parts, TOK // parts) for n in range(parts)]
        reads = [pltpu.make_async_copy(source.at[r], held.at[r], came.at[n]) for n, r in enumerate(rows)]
        writes = [pltpu.make_async_copy(held.at[r], dest.at[r], left.at[n]) for n, r in enumerate(rows)]
        for copy in reads:
            copy.start()
        for read, write in zip(reads, writes):
            read.wait()
            write.start()
        for copy in writes:
            copy.wait()

    return pl.pallas_call(
        hand_over,
        out_shape=jax.ShapeDtypeStruct((TOK, NY * QCOL), bf16),
        in_specs=[pl.BlockSpec(memory_space=pl.ANY)],
        out_specs=pl.BlockSpec(memory_space=pl.ANY),
        scratch_shapes=[pltpu.VMEM((TOK, NY * QCOL), bf16), dma((parts,)), dma((parts,))],
        compiler_params=pltpu.CompilerParams(vmem_limit_bytes=60 * 1024 * 1024),
    )(attended)


def solution(mesh):
    placed = (P(("ctx", "fsdp"), None), P(("ctx", "fsdp"), None), P(None, "fsdp", None, None), P())
    return jax.shard_map(
        shards, mesh=mesh, in_specs=placed, out_specs=P(("ctx", "fsdp"), None), check_vma=False
    )
```

```python
import math

import jax
import jax.numpy as jnp
from jax import lax
from jax.experimental import pallas as pl
from jax.experimental.pallas import tpu as pltpu
from jax.sharding import PartitionSpec as P

BLOCK = 128
RAND = 3
NX, NZ, NY = 4, 8, 4
N_CTX = NX * NZ * 2
SHARD = 16
HEAD = 128
MODEL = 4096
TOK = 512
GROUP = 4
ROW = 2 * HEAD
QCOL = GROUP * HEAD
QUARTER = MODEL // 4
SUB = QUARTER // 4
SLOTS = 61
EXP2_SCALE = math.log2(math.e) / math.sqrt(HEAD)
NT = (((1,), (1,)), ((), ()))


def kernel(
    listed, acts, queries, weight, out,
    acts_v, wbuf, kv_send, kv, kvw, glob, before, after,
    stage, pool, qx, acc, top, total, outbox, table, pairs, rand,
    loc, wy_s, wy_r, wd_s, wd_r, wx_s, wx_r, kv_s, kv_r, q_s, q_r,
    m_s, m_r, st_s, pool_r, halo_s, halo_r, g_s, g_r, out_s, out_r, near_by,
):
    c = lax.axis_index("ctx")
    y = lax.axis_index("fsdp")
    x = c // (2 * NZ)
    z = (c // 2) % NZ
    k = c % 2
    parity = (x + z) % 2

    def at(dx, dz, dk):
        return (((x + dx) % NX) * NZ + (z + dz) % NZ) * 2 + (k + dk) % 2

    def remote(src, dst, send, recv, ctx, head):
        return pltpu.make_async_remote_copy(
            src_ref=src, dst_ref=dst, send_sem=send, recv_sem=recv,
            device_id=(ctx, head), device_id_type=pl.DeviceIdType.MESH,
        )

    def peer(off):
        return (y + off) % NY

    sends = []

    def go(copy):
        copy.start()
        sends.append(copy)

    mine = (parity * 2 + k) * QUARTER
    other = ((1 - parity) * 2 + k) * QUARTER
    whole = pl.ds(mine, QUARTER)
    first = pl.ds(mine, QUARTER // 2)
    second = pl.ds(mine + QUARTER // 2, QUARTER // 2)
    barrier = pltpu.get_barrier_semaphore()

    def greet(ctx, head):
        pl.semaphore_signal(barrier, inc=1, device_id=(ctx, head), device_id_type=pl.DeviceIdType.MESH)

    for off in range(1, NY):
        greet(c, peer(off))
    along = (1, NZ - 1, 2, NZ - 2, 3, NZ - 3)
    for dz in along:
        greet(at(0, dz, 0), y)
    for n in range(1, 8):
        greet(at(n // 2, 0, n % 2), y)
    named = pltpu.make_async_copy(listed, rand, loc.at[3])
    named.start()
    own_w = pltpu.make_async_copy(weight, pairs, loc.at[1])
    own_w.start()
    own_q = pltpu.make_async_copy(
        queries.at[:, pl.ds(pl.multiple_of(y * QCOL, QCOL), QCOL)],
        qx.at[pl.ds(y * TOK, TOK)], loc.at[2],
    )
    acts_in = pltpu.make_async_copy(acts, acts_v, loc.at[0])
    acts_in.start()
    own_q.start()
    own_w.wait()

    line = lax.broadcasted_iota(jnp.int32, (2 * BLOCK, 2 * BLOCK), 0)
    place = lax.broadcasted_iota(jnp.int32, (2 * BLOCK, 2 * BLOCK), 1)
    wanted = jnp.where(line < BLOCK, 2 * line, 2 * (line - BLOCK) + 1)
    order = jnp.where(place == wanted, 1.0, 0.0).astype(jnp.bfloat16)

    def set_apart(b, _):
        parts = jnp.dot(order, pairs[pl.ds(b * ROW, ROW)], preferred_element_type=jnp.float32)
        parts = parts.astype(jnp.bfloat16)
        rows = pl.ds(b * BLOCK, BLOCK)
        wbuf[y, rows, 0:HEAD] = parts[0:BLOCK]
        wbuf[y, rows, HEAD:ROW] = parts[BLOCK:2 * BLOCK]
        return 0

    lax.fori_loop(0, MODEL // BLOCK, set_apart, 0, unroll=4)
    pl.semaphore_wait(barrier, 16)
    for n, (off, rows) in enumerate(((1, first), (3, second), (1, second), (3, first))):
        go(remote(wbuf.at[y, rows], wbuf.at[y, rows], wy_s.at[n], wy_r.at[n], c, peer(off)))
    for dz in along:
        pl.semaphore_signal(near_by, inc=1, device_id=(at(0, dz, 0), y), device_id_type=pl.DeviceIdType.MESH)
    acts_in.wait()
    named.wait()

    def project(head, dest, lead):
        def tile(t, _):
            rows = pl.ds(t * 256, 256)
            total_ = jnp.dot(acts_v[rows, 0:1024], wbuf[head, 0:1024],
                             preferred_element_type=jnp.float32)
            for u in range(1, 4):
                total_ += jnp.dot(acts_v[rows, u * 1024:(u + 1) * 1024],
                                  wbuf[head, u * 1024:(u + 1) * 1024],
                                  preferred_element_type=jnp.float32)
            dest[pl.ds(lead + t * 2, 2)] = total_.astype(jnp.bfloat16).reshape(2, BLOCK, ROW)
            return 0
        lax.fori_loop(0, 2, tile, 0)

    project(y, kv, y * 4)

    offs = (1, 3, 2)

    def landed(view, send, recv):
        remote(view, view, send, recv, at(0, 0, 1), y).wait_recv()

    below, above = at(0, NZ - 1, 0), at(0, 1, 0)

    def in_plane(n):
        return at(n // 2, 0, n % 2)

    groups = {
        "own": (c, 0, 1, 8, in_plane),
        "below 3": (below, 7, 0, 4, lambda n: at(n, 3, 0)),
        "above 3": (above, 11, 0, 4, lambda n: at(n, NZ - 3, 1)),
        "below": (below, 47, 1, 8, in_plane),
        "above": (above, 54, 1, 8, in_plane),
        "below 2": (below, 15, 0, 8, lambda n: at(n // 2, 2, n % 2)),
        "above 2": (above, 23, 0, 8, lambda n: at(n // 2, NZ - 2, n % 2)),
        "below 1": (below, 31, 0, 8, lambda n: at(n // 2, 1, n % 2)),
        "above 1": (above, 39, 0, 8, lambda n: at(n // 2, NZ - 1, n % 2)),
    }
    keep = {"own": 61, "below": 62, "above": 63}

    def named_block(dst, source):
        found = jnp.int32(0)
        for r in range(RAND):
            for b in range(SHARD):
                v = rand[r, dst * SHARD + b]
                found += jnp.where(v >> 4 == source, v & 15, 0)
        return found

    def look_up(name):
        source, base, lo, hi, dest_of = groups[name]

        def body(n, _):
            table[base + n - lo] = named_block(dest_of(n), source)
            return 0

        lax.fori_loop(lo, hi, body, 0)
        if name in keep:
            table[keep[name]] = named_block(c, source)

    def pick(name, buffer):
        source, base, lo, hi, dest_of = groups[name]
        if name in keep:
            pool[source] = buffer[table[keep[name]]]

        def body(n, _):
            slot = base + n - lo
            stage[slot] = buffer[table[slot]]
            remote(stage.at[slot], pool.at[source], st_s, pool_r, dest_of(n), y).start()
            return 0

        lax.fori_loop(lo, hi, body, 0)

    def multicast(n, head):
        rows = pl.ds(head * 4, 4)
        go(remote(kv.at[rows], before.at[rows], m_s.at[0, n], m_r.at[0, n], at(0, 1, 0), y))
        go(remote(kv.at[rows], after.at[rows], m_s.at[1, n], m_r.at[1, n], at(0, -1 + NZ, 0), y))

    def to_sibling(n, off):
        head = peer(off)
        go(remote(wbuf.at[head, whole], wbuf.at[head, whole], wd_s.at[0, n], wd_r.at[0, n],
                  at(0, 0, 1), y))

    def to_chips(n, off, part):
        head = peer(off)
        steps = ((1, 0), (NX - 1, 0), (0, 1), (0, NZ - 1))
        for j in (2 * part, 2 * part + 1):
            dx, dz = steps[j]
            rows = pl.ds(mine + j * SUB, SUB)
            go(remote(wbuf.at[head, rows], wbuf.at[head, rows], wx_s.at[n, j], wx_r.at[n, j],
                      at(dx, dz, 0), y))

    multicast(0, y)
    for name in groups:
        look_up(name)

    landed(wbuf.at[peer(3), first], wy_s.at[0], wy_r.at[0])
    go(remote(wbuf.at[peer(3), first], wbuf.at[peer(3), first], wy_s.at[4], wy_r.at[4], c, peer(1)))
    to_chips(1, 3, 0)
    landed(wbuf.at[peer(1), second], wy_s.at[1], wy_r.at[1])
    go(remote(wbuf.at[peer(1), second], wbuf.at[peer(1), second], wy_s.at[5], wy_r.at[5], c, peer(3)))
    to_chips(0, 1, 1)
    landed(wbuf.at[peer(3), second], wy_s.at[2], wy_r.at[2])
    to_chips(1, 3, 1)
    to_sibling(1, 3)
    landed(wbuf.at[peer(1), first], wy_s.at[3], wy_r.at[3])
    to_chips(0, 1, 0)
    to_sibling(0, 1)

    far = pl.ds(other, QUARTER)
    sib_mine = pl.ds((parity * 2 + 1 - k) * QUARTER, QUARTER)
    sib_other = pl.ds(((1 - parity) * 2 + 1 - k) * QUARTER, QUARTER)

    def pass_far(n, off):
        head = peer(off)
        for j in range(4):
            landed(wbuf.at[head, pl.ds(other + j * SUB, SUB)], wx_s.at[n, j], wx_r.at[n, j])
        go(remote(wbuf.at[head, far], wbuf.at[head, far], wd_s.at[1, n], wd_r.at[1, n],
                  at(0, 0, 1), y))

    def serve(n, off):
        head = peer(off)
        landed(wbuf.at[head, sib_mine], wd_s.at[0, n], wd_r.at[0, n])
        landed(wbuf.at[head, sib_other], wd_s.at[1, n], wd_r.at[1, n])
        project(head, kv_send.at[n], 0)
        go(remote(kv_send.at[n], kv.at[pl.ds(y * 4, 4)], kv_s.at[n], kv_r.at[n], c, head))

    pass_far(0, 1)
    pass_far(1, 3)
    landed(wbuf.at[peer(2), first], wy_s.at[4], wy_r.at[4])
    to_chips(2, 2, 0)
    landed(wbuf.at[peer(2), second], wy_s.at[5], wy_r.at[5])
    to_chips(2, 2, 1)
    to_sibling(2, 2)
    serve(0, 1)
    serve(1, 3)
    pass_far(2, 2)
    serve(2, 2)

    to_glob = pltpu.make_async_copy(kv.at[pl.ds(0, 2)], glob, loc.at[4])

    def root_copies():
        return [remote(kv.at[pl.ds(0, 2)], glob, g_s.at[n], g_r, at(0, dz, 0), y)
                for n, dz in enumerate((2, NZ - 2, 1, NZ - 1))]

    def up_copies():
        return [remote(glob, glob, g_s.at[4 + n], g_r, at(0, dz, 0), y) for n, dz in enumerate((2, 1))]

    def down_copies():
        return [remote(glob, glob, g_s.at[6], g_r, at(0, NZ - 1, 0), y)]

    def plane_copies():
        return [remote(glob, glob, g_s.at[6 + j], g_r, at(j // 2, 0, j % 2), y) for j in range(1, 8)]

    on_line = jnp.logical_and(x == 0, k == 0)
    tree = (
        (jnp.logical_and(on_line, z == 2), up_copies),
        (jnp.logical_and(on_line, z == NZ - 2), down_copies),
        (on_line, plane_copies),
    )

    def send_globals(holder):
        @pl.when(jnp.logical_and(c == 0, holder == 0))
        def _():
            for copy in root_copies():
                copy.start()
            to_glob.start()

    send_globals(y)

    for n, off in enumerate(offs):
        head = peer(NY - off)
        landed(kv.at[pl.ds(head * 4, 4)], kv_s.at[n], kv_r.at[n])
        send_globals(head)
        multicast(n + 1, head)

    go(remote(kv.at[SHARD - 1], kvw.at[0], halo_s.at[0], halo_r.at[0], (c + 1) % N_CTX, y))
    go(remote(kv.at[0], kvw.at[SHARD + 1], halo_s.at[1], halo_r.at[1], (c + N_CTX - 1) % N_CTX, y))
    to_window = pltpu.make_async_copy(kv, kvw.at[pl.ds(1, SHARD)], loc.at[3])
    to_window.start()
    for n, off in enumerate(offs):
        head = peer(off)
        go(remote(queries.at[:, pl.ds(pl.multiple_of(head * QCOL, QCOL), QCOL)],
                  qx.at[pl.ds(y * TOK, TOK)], q_s.at[n], q_r.at[n], c, head))

    pick("own", kv)

    @pl.when(c == 0)
    def _():
        to_glob.wait()

    @pl.when(jnp.logical_and(on_line, c != 0))
    def _():
        landed(glob, g_s.at[0], g_r)

    for holds, copies in tree:
        @pl.when(holds)
        def _():
            for copy in copies():
                copy.start()

    for n, off in enumerate((0, *offs)):
        rows = pl.ds(peer(NY - off) * 4, 4)
        landed(before.at[rows], m_s.at[0, n], m_r.at[0, n])
        landed(after.at[rows], m_s.at[1, n], m_r.at[1, n])
    pl.semaphore_wait(near_by, len(along))
    for name in groups:
        if name != "own":
            pick(name, before if name.startswith("below") else after)

    @pl.when(jnp.logical_not(on_line))
    def _():
        landed(glob, g_s.at[0], g_r)

    to_window.wait()
    landed(kvw.at[0], halo_s.at[0], halo_r.at[0])
    landed(kvw.at[SHARD + 1], halo_s.at[1], halo_r.at[1])
    own_q.wait()
    for n, off in enumerate(offs):
        landed(qx.at[pl.ds(peer(NY - off) * TOK, TOK)], q_s.at[n], q_r.at[n])

    half = GROUP // 2

    def stacked(i, part):
        rows = pl.ds(i * BLOCK, BLOCK)
        return jnp.concatenate(
            [qx[rows, g * HEAD:(g + 1) * HEAD] for g in range(part * half, (part + 1) * half)], axis=0
        )

    def near(i, _):
        keys = jnp.concatenate(
            [kvw[pl.ds(i, 3), :, 0:HEAD].reshape(3 * BLOCK, HEAD),
             glob[:, :, 0:HEAD].reshape(2 * BLOCK, HEAD)], axis=0)
        values = jnp.concatenate(
            [kvw[pl.ds(i, 3), :, HEAD:ROW].reshape(3 * BLOCK, HEAD),
             glob[:, :, HEAD:ROW].reshape(2 * BLOCK, HEAD)], axis=0)
        for part in range(2):
            rows = slice(part * half * BLOCK, (part + 1) * half * BLOCK)
            scores = lax.dot_general(stacked(i, part), keys, NT, preferred_element_type=jnp.float32)
            largest = jnp.max(scores, axis=-1, keepdims=True)
            weights = jnp.exp2((scores - largest) * EXP2_SCALE)
            top[i, rows] = largest
            total[i, rows] = jnp.sum(weights, axis=-1, keepdims=True)
            acc[i, rows] = jnp.dot(weights.astype(jnp.bfloat16), values,
                                   preferred_element_type=jnp.float32)
        return 0

    lax.fori_loop(0, SHARD, near, 0)

    landed(pool.at[pl.ds(0, SLOTS)], st_s, pool_r)

    def out_copy(j, i):
        column = pl.ds(pl.multiple_of(y * QCOL, QCOL), QCOL)
        return remote(outbox.at[pl.ds(i * BLOCK, BLOCK)],
                      out.at[pl.ds((i % 4) * BLOCK, BLOCK), column],
                      out_s.at[j], out_r.at[j], c, i // 4)

    def out_local(j, i):
        column = pl.ds(pl.multiple_of(y * QCOL, QCOL), QCOL)
        return pltpu.make_async_copy(outbox.at[pl.ds(i * BLOCK, BLOCK)],
                                     out.at[pl.ds((i % 4) * BLOCK, BLOCK), column], out_s.at[j])

    def block_of(j):
        step = j // 4
        off = jnp.where(step < 2, 2 - step, (3 - step) * 3)
        return ((y + off) % NY) * 4 + j % 4

    def finish(j, _):
        i = block_of(j)
        chosen = [pool[rand[r, c * SHARD + i] >> 4] for r in range(RAND)]
        keys = jnp.concatenate([b[:, 0:HEAD] for b in chosen], axis=0)
        values = jnp.concatenate([b[:, HEAD:ROW] for b in chosen], axis=0)
        for part in range(2):
            rows = slice(part * half * BLOCK, (part + 1) * half * BLOCK)
            scores = lax.dot_general(stacked(i, part), keys, NT, preferred_element_type=jnp.float32)
            early = top[i, rows]
            largest = jnp.maximum(early, jnp.max(scores, axis=-1, keepdims=True))
            weights = jnp.exp2((scores - largest) * EXP2_SCALE)
            fade = jnp.exp2((early - largest) * EXP2_SCALE)
            mass = total[i, rows] * fade + jnp.sum(weights, axis=-1, keepdims=True)
            mixed = acc[i, rows] * fade + jnp.dot(weights.astype(jnp.bfloat16), values,
                                                  preferred_element_type=jnp.float32)
            result = (mixed / mass).astype(jnp.bfloat16)
            for g in range(half):
                column = (part * half + g) * HEAD
                outbox[pl.ds(i * BLOCK, BLOCK), column:column + HEAD] = result[g * BLOCK:(g + 1) * BLOCK]

        @pl.when(j < 12)
        def _():
            out_copy(j, i).start()

        @pl.when(j >= 12)
        def _():
            out_local(j, i).start()
        return 0

    lax.fori_loop(0, 16, finish, 0)

    for copy in sends:
        copy.wait_send()

    for holds, copies in ((c == 0, root_copies), *tree):
        @pl.when(holds)
        def _():
            for copy in copies():
                copy.wait_send()

    everything = stage.at[pl.ds(0, SLOTS)]
    remote(everything, pool.at[pl.ds(0, SLOTS)], st_s, pool_r, at(0, 0, 1), y).wait_send()

    def drain(j, _):
        i = block_of(j)

        @pl.when(j < 12)
        def _():
            out_copy(j, i).wait()

        @pl.when(j >= 12)
        def _():
            out_local(j, i).wait()
        return 0

    lax.fori_loop(0, 16, drain, 0)


def shards(acts, queries, kv_weight, rand_blocks):
    flat_weight = kv_weight.reshape(2 * MODEL, HEAD)
    bf16, f32 = jnp.bfloat16, jnp.float32
    blocks = pltpu.VMEM((SHARD, BLOCK, ROW), bf16)
    dma = pltpu.SemaphoreType.DMA
    attended = pl.pallas_call(
        kernel,
        out_shape=jax.ShapeDtypeStruct((TOK, NY * QCOL), bf16),
        in_specs=[pl.BlockSpec(memory_space=pl.ANY)] * 4,
        out_specs=pl.BlockSpec(memory_space=pl.ANY),
        scratch_shapes=[
            pltpu.VMEM((TOK, MODEL), bf16),
            pltpu.VMEM((NY, MODEL, ROW), bf16),
            pltpu.VMEM((3, 4, BLOCK, ROW), bf16),
            blocks,
            pltpu.VMEM((SHARD + 2, BLOCK, ROW), bf16),
            pltpu.VMEM((2, BLOCK, ROW), bf16),
            blocks, blocks,
            pltpu.VMEM((SLOTS, BLOCK, ROW), bf16),
            pltpu.VMEM((N_CTX, BLOCK, ROW), bf16),
            pltpu.VMEM((NY * TOK, QCOL), bf16),
            pltpu.VMEM((SHARD, GROUP * BLOCK, HEAD), f32),
            pltpu.VMEM((SHARD, GROUP * BLOCK, 1), f32),
            pltpu.VMEM((SHARD, GROUP * BLOCK, 1), f32),
            pltpu.VMEM((NY * TOK, QCOL), bf16),
            pltpu.SMEM((N_CTX,), jnp.int32),
            pltpu.VMEM((2 * MODEL, HEAD), bf16),
            pltpu.SMEM((RAND, N_CTX * SHARD), jnp.int32),
            dma((5,)), dma((6,)), dma((6,)), dma((2, 3)), dma((2, 3)), dma((3, 4)), dma((3, 4)),
            dma((3,)), dma((3,)), dma((3,)), dma((3,)),
            dma((2, 4)), dma((2, 4)), dma, dma, dma((2,)), dma((2,)), dma((14,)), dma,
            dma((16,)), dma((16,)), pltpu.SemaphoreType.REGULAR,
        ],
        compiler_params=pltpu.CompilerParams(
            collective_id=0, has_side_effects=True, vmem_limit_bytes=60 * 1024 * 1024
        ),
        cost_estimate=pl.CostEstimate(
            flops=9 * 10**9, bytes_accessed=12 * 2**20, transcendentals=8 * 2**20
        ),
    )(rand_blocks.T, acts, queries, flat_weight)
    parts = 8

    def hand_over(source, dest, held, came, left):
        rows = [pl.ds(n * TOK // parts, TOK // parts) for n in range(parts)]
        reads = [pltpu.make_async_copy(source.at[r], held.at[r], came.at[n]) for n, r in enumerate(rows)]
        writes = [pltpu.make_async_copy(held.at[r], dest.at[r], left.at[n]) for n, r in enumerate(rows)]
        for copy in reads:
            copy.start()
        for read, write in zip(reads, writes):
            read.wait()
            write.start()
        for copy in writes:
            copy.wait()

    return pl.pallas_call(
        hand_over,
        out_shape=jax.ShapeDtypeStruct((TOK, NY * QCOL), bf16),
        in_specs=[pl.BlockSpec(memory_space=pl.ANY)],
        out_specs=pl.BlockSpec(memory_space=pl.ANY),
        scratch_shapes=[pltpu.VMEM((TOK, NY * QCOL), bf16), dma((parts,)), dma((parts,))],
        compiler_params=pltpu.CompilerParams(vmem_limit_bytes=60 * 1024 * 1024),
    )(attended)


def solution(mesh):
    placed = (P(("ctx", "fsdp"), None), P(("ctx", "fsdp"), None), P(None, "fsdp", None, None), P())
    return jax.shard_map(
        shards, mesh=mesh, in_specs=placed, out_specs=P(("ctx", "fsdp"), None), check_vma=False
    )
```
